256 devices in a mesh: member: 4 (over y_lo, core), tile: 64 (over z, x, y_hi).
Axes of the slice: x: 4, y: 4 (y_hi: 2, y_lo: 2; y = y_hi * 2 + y_lo), z: 8, core: 2. Of those that a mesh axis runs over, the one named last changes fastest.
Arguments:
- initial: float32 [4, 8, 1024, 1024], P('member', None, 'tile'), may hold values from -6 to 6
- target: float32 [8, 1024, 1024], P(None, 'tile'), may hold values from -6 to 6
- noise: bfloat16 [2, 4, 8, 1024, 1024], P(None, 'member', None, 'tile'), may hold values from -6 to 6
- w_qkv: bfloat16 [1024, 3072], replicated, may hold values from -0.1875 to 0.1875
- w_out: bfloat16 [1024, 1024], replicated, may hold values from -0.1875 to 0.1875
- gain: float32 [1024], replicated, may hold values from 0.5 to 1.5
- noise_scale: float32 [1024], replicated, may hold values from 0.3 to 1
- shifts: int32 [2, 2], replicated, may hold values from 1 to 7
Outputs:
- state_grad: float32 [4, 8, 1024, 1024], P('member', None, 'tile')
- gain_grad: float32 [1024], replicated
- scale_grad: float32 [1024], replicated
The draws below stay inside these ranges and needn't reach their ends.
Inputs may be any that keep to these rules, and one draw needn't show every extreme that they name: `shifts`: each step's offsets of the window grid, in cells.
All inputs are finite; a program needn't handle non-finite values.
Results may differ from the reference program's by a relative error of at most 0.025.
Values may be sent and summed in bfloat16 or wider, within the bound.
No kernel may reach another device: no remote copies, remote signals or barrier semaphores. Data moves between devices by JAX's collectives and lax.ppermute only.
A program may use at most 128 MiB of HBM per device.

```python
import math
import jax
import jax.numpy as jnp
from jax import lax

C = 1024
HEAD = 32
WIN = 8
STEPS = 2
LAT = 8
M = 4
LON = 1024


def with_ends(entries, rng, least, largest):
    dims = entries.shape
    place = [jax.random.randint(jax.random.fold_in(rng, axis), (), 0, dims[axis]) for axis in range(len(dims))]
    entries = entries.at[tuple(place)].set(least)
    longest = dims.index(max(dims))
    place[longest] = (place[longest] + 1) % dims[longest]
    return entries.at[tuple(place)].set(largest)


def level_of(own_key, dims, shards, low, top_value):
    level = 1.0
    for axis_at, shards_of in shards:
        steps = jax.random.uniform(jax.random.fold_in(jax.random.fold_in(own_key, 6), axis_at), (shards_of,), jnp.float32, low / len(shards), top_value / len(shards))
        level = level * jnp.repeat(jnp.exp(steps), dims[axis_at] // shards_of).reshape((-1,) + (1,) * (len(dims) - 1 - axis_at))
    return level


def normal_values(stream_key, extent, scale, reach, pieces=(), held_as=jnp.bfloat16):
    values = scale * jax.random.normal(stream_key, extent, jnp.float32)
    if pieces:
        values = values * level_of(stream_key, extent, pieces, -0.22, 0.18)
    return jnp.clip(values, -reach, reach).astype(held_as)


def setup_inputs(seed: int = 0) -> dict:
    key_of = jax.random.split(jax.random.key(seed), 9)
    return {
        "initial": normal_values(key_of[0], (M, LAT, LON, C), 1.0, 6.0, ((0, 4), (2, 64)), jnp.float32),
        "target": normal_values(key_of[1], (LAT, LON, C), 1.0, 6.0, ((1, 64),), jnp.float32),
        "noise": normal_values(key_of[2], (STEPS, M, LAT, LON, C), 1.0, 6.0, ((1, 4), (3, 64))),
        "w_qkv": normal_values(key_of[3], (C, 3 * C), C ** -0.5, 0.1875),
        "w_out": normal_values(key_of[4], (C, C), C ** -0.5, 0.1875),
        "gain": jnp.clip(1.0 + 0.1 * jax.random.normal(key_of[5], (C,), jnp.float32), 0.5, 1.5),
        "noise_scale": jnp.clip(jnp.exp(jax.random.uniform(key_of[6], (C,), jnp.float32, math.log(0.3), math.log(1.0))), 0.3, 1.0),
        "shifts": with_ends(jax.random.randint(key_of[7], (STEPS, 2), 1, WIN), jax.random.fold_in(key_of[7], 1), 1, WIN - 1).astype(jnp.int32),
    }


smoothing = 0.25

def product(form, left, right):
    return jnp.einsum(form, left.astype(jnp.float32), right.astype(jnp.float32))

def normalize(fields, gain):
    centre = lax.optimization_barrier(jnp.mean(fields, axis=-1, keepdims=True))
    offset = fields - centre
    spread = lax.rsqrt(lax.optimization_barrier(jnp.mean(offset * offset, axis=-1, keepdims=True)) + 1e-05)
    scaled = offset * spread
    return (scaled, spread, (scaled * gain).astype(jnp.bfloat16))

def normalize_back(d_normed, scaled, spread, gain):
    d_hat = d_normed * gain
    d_fields = spread * (d_hat - lax.optimization_barrier(jnp.mean(d_hat, axis=-1, keepdims=True)) - scaled * lax.optimization_barrier(jnp.mean(d_hat * scaled, axis=-1, keepdims=True)))
    return (d_fields, lax.optimization_barrier(jnp.sum(d_normed * scaled, axis=(0, 1, 2))))

def to_windows(fields, lat_shift):
    rolled = jnp.roll(fields, -lat_shift, axis=1)
    members, height, columns, channels = rolled.shape
    blocks = rolled.reshape(members, height // WIN, WIN, columns // WIN, WIN, channels)
    return blocks.transpose(0, 1, 3, 2, 4, 5).reshape(-1, WIN * WIN, channels)

def from_windows(windows, lat_shift, members, height, columns):
    channels = windows.shape[-1]
    blocks = windows.reshape(members, height // WIN, columns // WIN, WIN, WIN, channels).transpose(0, 1, 3, 2, 4, 5)
    return jnp.roll(blocks.reshape(members, height, columns, channels), lat_shift, axis=1)

def window_mask(lat_shift, members, height, columns):
    row_wins = height // WIN
    col_wins = columns // WIN
    inside = jnp.arange(WIN * WIN, dtype=jnp.int32) // WIN
    row_index = jnp.arange(row_wins, dtype=jnp.int32)[:, None] * WIN + inside[None, :]
    region = row_index >= height - lat_shift
    allowed = region[:, :, None] == region[:, None, :]
    allowed = jnp.broadcast_to(allowed[None, :, None], (members, row_wins, col_wins, WIN * WIN, WIN * WIN))
    return allowed.reshape(-1, WIN * WIN, WIN * WIN)

def attend(normed, w_qkv, w_out, allowed):
    windows, tokens, channels = normed.shape
    head_count = channels // HEAD
    packed = jnp.dot(normed.reshape(-1, channels), w_qkv, preferred_element_type=jnp.float32).astype(jnp.bfloat16)
    packed = packed.reshape(windows, tokens, 3, head_count, HEAD)
    queries = packed[:, :, 0]
    keys_all = packed[:, :, 1]
    values = packed[:, :, 2]
    scores = product('wqhd,wkhd->whqk', queries, keys_all) * HEAD ** (-0.5)
    scores = jnp.where(allowed[:, None], scores, -1000000000.0)
    highest = lax.optimization_barrier(jnp.max(scores, axis=-1, keepdims=True))
    raised = jnp.exp(scores - highest)
    probs_all = raised / lax.optimization_barrier(jnp.sum(raised, axis=-1, keepdims=True))
    weights = probs_all.astype(jnp.bfloat16)
    mixed_rows = product('whqk,wkhd->wqhd', weights, values).astype(jnp.bfloat16).reshape(-1, channels)
    branch = jnp.dot(mixed_rows, w_out, preferred_element_type=jnp.float32).reshape(windows, tokens, channels)
    return (branch, (queries, keys_all, values, probs_all, weights))

def attend_back(d_branch, saved, w_qkv, w_out):
    queries, keys_all, values, probs_all, weights = saved
    windows, tokens, channels = d_branch.shape
    head_count = channels // HEAD
    flat_rows = d_branch.astype(jnp.bfloat16).reshape(-1, channels)
    d_mixed = lax.dot_general(flat_rows, w_out, (((1,), (1,)), ((), ())), preferred_element_type=jnp.float32)
    d_mixed = d_mixed.astype(jnp.bfloat16).reshape(windows, tokens, head_count, HEAD)
    d_weights = product('wqhd,wkhd->whqk', d_mixed, values)
    d_values = product('whqk,wqhd->wkhd', weights, d_mixed).astype(jnp.bfloat16)
    centred = d_weights - lax.optimization_barrier(jnp.sum(d_weights * probs_all, axis=-1, keepdims=True))
    d_scores = (probs_all * centred * HEAD ** (-0.5)).astype(jnp.bfloat16)
    d_queries = product('whqk,wkhd->wqhd', d_scores, keys_all).astype(jnp.bfloat16)
    d_keys = product('whqk,wqhd->wkhd', d_scores, queries).astype(jnp.bfloat16)
    d_packed = jnp.stack([d_queries, d_keys, d_values], axis=2).reshape(-1, 3 * channels)
    d_normed = lax.dot_general(d_packed, w_qkv, (((1,), (1,)), ((), ())), preferred_element_type=jnp.float32)
    return d_normed.reshape(windows, tokens, channels)

def step_forward(fields, noise_now, gain, noise_scale, w_qkv, w_out, lat_shift, lon_shift):
    scaled, spread, normed = normalize(fields, gain)
    shifted = jnp.roll(normed, -lon_shift, axis=2)
    allowed = window_mask(lat_shift, 1, LAT, LON)
    branch, saved = attend(to_windows(shifted, lat_shift), w_qkv, w_out, allowed)
    branch = jnp.roll(from_windows(branch, lat_shift, 1, LAT, LON), lon_shift, axis=2)
    following = fields + branch + noise_scale * noise_now.astype(jnp.float32)
    return (following, (scaled, spread, saved))

def step_backward(d_next, noise_now, memory, gain, w_qkv, w_out, lat_shift, lon_shift):
    scaled, spread, saved = memory
    shifted = jnp.roll(d_next, -lon_shift, axis=2)
    d_windows = attend_back(to_windows(shifted, lat_shift), saved, w_qkv, w_out)
    d_normed = jnp.roll(from_windows(d_windows, lat_shift, 1, LAT, LON), lon_shift, axis=2)
    d_fields, gain_term = normalize_back(d_normed, scaled, spread, gain)
    scale_term = lax.optimization_barrier(jnp.sum(d_next * noise_now.astype(jnp.float32), axis=(0, 1, 2)))
    return (d_next + d_fields, gain_term, scale_term)

def slope(difference):
    return difference * lax.rsqrt(difference * difference + smoothing * smoothing)

def crps_seed(final, target):

    def one_member(fields):
        pair_sums = lax.optimization_barrier(jnp.sum(slope(fields[None] - final), axis=0))
        return slope(fields - target) - pair_sums / (M - 1)
    return lax.map(one_member, final)

def reference(initial, target, noise, w_qkv, w_out, gain, noise_scale, shifts):
    by_member = jnp.swapaxes(noise, 0, 1)

    def roll_out(inputs):
        fields, member_noise = inputs
        fields = fields[None]
        for step_index in range(STEPS):
            fields, memory = step_forward(fields, member_noise[step_index][None], gain, noise_scale, w_qkv, w_out, shifts[step_index, 0], shifts[step_index, 1])
        return fields[0]
    final = lax.map(roll_out, (initial, by_member))
    seed_fields = crps_seed(final, target)

    def member_back(inputs):
        fields, member_noise, seed_now = inputs
        fields = fields[None]
        memories = []
        for step_index in range(STEPS):
            fields, memory = step_forward(fields, member_noise[step_index][None], gain, noise_scale, w_qkv, w_out, shifts[step_index, 0], shifts[step_index, 1])
            memories.append(memory)
        d_fields = seed_now[None]
        gain_total = jnp.zeros((C,), jnp.float32)
        scale_total = jnp.zeros((C,), jnp.float32)
        for step_index in reversed(range(STEPS)):
            d_fields, gain_term, scale_term = step_backward(d_fields, member_noise[step_index][None], memories[step_index], gain, w_qkv, w_out, shifts[step_index, 0], shifts[step_index, 1])
            gain_total = gain_total + gain_term
            scale_total = scale_total + scale_term
        return (d_fields[0], gain_total, scale_total)
    state_grad, gain_terms, scale_terms = lax.map(member_back, (initial, by_member, seed_fields))
    factor = (M * LAT * LON) ** (-0.5)
    return (state_grad, lax.optimization_barrier(jnp.sum(gain_terms, axis=0)) * factor, lax.optimization_barrier(jnp.sum(scale_terms, axis=0)) * factor)
```

```python
import functools

import jax
import jax.numpy as jnp
from jax import lax
from jax.experimental import pallas as pl
from jax.experimental.pallas import tpu as pltpu
from jax.sharding import PartitionSpec as P

C = 1024
HEAD = 32
WIN = 8
LAT = 8
TOK = LAT * WIN
GROUP = 4
LANES = GROUP * HEAD
GROUPS = C // LANES
SPAN = GROUP * TOK
SCALE = HEAD ** (-0.5)
SMOOTH = 0.25
F32 = jnp.float32
BF16 = jnp.bfloat16
VMEM_LIMIT = 40 * 1024 * 1024


def dot(left, right):
    return lax.dot_general(left, right, (((1,), (0,)), ((), ())), preferred_element_type=F32)


def dot_nt(left, right):
    return lax.dot_general(left, right, (((1,), (1,)), ((), ())), preferred_element_type=F32)


def dot_tn(left, right):
    return lax.dot_general(left, right, (((0,), (0,)), ((), ())), preferred_element_type=F32)


def head_masks():
    lane = lax.broadcasted_iota(jnp.int32, (TOK, LANES), 1) // HEAD
    return [lane == head for head in range(GROUP)]


def by_head(value, masks):
    zero = jnp.zeros_like(value)
    return jnp.concatenate([jnp.where(mask, value, zero) for mask in masks], axis=0)


def fold_heads(stacked, masks):
    out = stacked[:TOK]
    for head in range(1, GROUP):
        out = jnp.where(masks[head], stacked[head * TOK : (head + 1) * TOK], out)
    return out


def lat_mask(lat_shift):
    key_lat = lax.broadcasted_iota(jnp.int32, (TOK, SPAN), 0) // WIN
    query_lat = (lax.broadcasted_iota(jnp.int32, (TOK, SPAN), 1) % TOK) // WIN
    return (key_lat < lat_shift) == (query_lat < lat_shift)


def lanes(start, size):
    return pl.ds(pl.multiple_of(start, 128), size)


def fill(ext, own_ref, west, east):
    for row in range(LAT):
        ext[row, 0:8, :] = west[row * WIN : (row + 1) * WIN]
        ext[row, 8:24, :] = own_ref[row].astype(F32)
        ext[row, 24:32, :] = east[row * WIN : (row + 1) * WIN]


def frame(ext, row, start, columns):
    return pltpu.roll(ext[row], lax.rem(32 - start, 32), 0)[:columns]


def norm_rows(x_ref, rows, gain, normed_ref, scaled_ref, spread_ref, saved_from):
    for at in range(0, rows, 32):
        x = x_ref[at : at + 32, :]
        centre = jnp.mean(x, axis=-1, keepdims=True)
        offset = x - centre
        spread = lax.rsqrt(jnp.mean(offset * offset, axis=-1, keepdims=True) + 1e-05)
        scaled = offset * spread
        normed_ref[at : at + 32, :] = (scaled * gain).astype(BF16)
        if at >= saved_from:
            scaled_ref[at - saved_from : at - saved_from + 32, :] = scaled
            spread_ref[at - saved_from : at - saved_from + 32, :] = jnp.broadcast_to(
                spread, (32, 128)
            )


def attend(windows, packed_ref, weights_ref, mixed_ref, lat_shift, saved_from):
    masks = head_masks()
    allowed = lat_mask(lat_shift)

    def group(at, _):
        for window in range(windows):
            rows = slice(window * TOK, (window + 1) * TOK)
            queries = packed_ref[rows, lanes(at * LANES, LANES)]
            keys = packed_ref[rows, lanes(C + at * LANES, LANES)]
            values = packed_ref[rows, lanes(2 * C + at * LANES, LANES)]
            scores = dot_nt(keys, by_head(queries, masks))
            scores = jnp.where(allowed, scores, -1e9 / SCALE)
            highest = jnp.max(scores, axis=0, keepdims=True)
            raised = jnp.exp((scores - highest) * SCALE)
            total = jnp.sum(raised, axis=0, keepdims=True)
            weights = (raised * (1.0 / total)).astype(BF16)
            if window >= saved_from:
                weights_ref[(window - saved_from) * GROUPS + at] = weights
            mixed = fold_heads(dot_tn(weights, values), masks)
            mixed_ref[rows, lanes(at * LANES, LANES)] = mixed.astype(BF16)
        return 0

    lax.fori_loop(0, GROUPS, group, 0)


def forward_kernel(
    shifts,
    initial,
    target,
    noise,
    east,
    west,
    gain,
    noise_scale,
    w_qkv_hbm,
    w_out_hbm,
    final_out,
    sent_out,
    target_out,
    noise_out,
    packed0_out,
    weights0_out,
    scaled0_out,
    spread0_out,
    packed1_out,
    weights1_out,
    scaled1_out,
    spread1_out,
    w_qkv,
    w_out,
    ext,
    state,
    normed,
    packed,
    mixed,
    sems,
):
    copies = []
    for part in range(6):
        at = pl.ds(part * 512, 512)
        copies.append(
            pltpu.make_async_copy(w_qkv_hbm.at[:, at], w_qkv.at[:, at], sems.at[part])
        )
    copies.append(pltpu.make_async_copy(w_out_hbm, w_out, sems.at[6]))
    for copy in copies:
        copy.start()
    lat0, lon0, lat1, lon1 = shifts[0, 0], shifts[0, 1], shifts[1, 0], shifts[1, 1]
    origin1 = jnp.where(lon1 <= lon0, lon1, lon1 - WIN)

    fill(ext, initial, west[0].astype(F32), east[0].astype(F32))
    for row in range(LAT):
        part = frame(ext, row, lon0, 24)
        for window in range(3):
            state[window * TOK + row * WIN : window * TOK + (row + 1) * WIN, :] = part[
                window * WIN : (window + 1) * WIN
            ]
    norm_rows(state, 3 * TOK, gain[...], normed, scaled0_out, spread0_out, TOK)
    for part in range(6):
        copies[part].wait()
        packed[:, part * 512 : (part + 1) * 512] = dot(
            normed[...], w_qkv[:, part * 512 : (part + 1) * 512]
        ).astype(BF16)
    packed0_out[...] = packed[TOK:, :]
    attend(3, packed, weights0_out, mixed, lat0, 1)
    copies[6].wait()
    for part in range(4):
        at = slice(part * 256, (part + 1) * 256)
        branch = dot(mixed[...], w_out[:, at])
        for row in range(LAT):
            for window in range(3):
                rows = slice(window * TOK + row * WIN, window * TOK + (row + 1) * WIN)
                ext[row, window * WIN : (window + 1) * WIN, at] = state[rows, at] + branch[rows]

    scale = noise_scale[...]
    for row in range(LAT):
        part = frame(ext, row, origin1 - lon0 + WIN, 16)
        for window in range(2):
            rows = slice(window * TOK + row * WIN, window * TOK + (row + 1) * WIN)
            state[rows, :] = part[window * WIN : (window + 1) * WIN]
    for step in range(2):
        fill(ext, noise.at[step], west[1 + step].astype(F32), east[1 + step].astype(F32))
        for row in range(LAT):
            part = frame(ext, row, origin1 + WIN, 16)
            for window in range(2):
                rows = slice(window * TOK + row * WIN, window * TOK + (row + 1) * WIN)
                here = part[window * WIN : (window + 1) * WIN]
                if step == 0:
                    state[rows, :] = state[rows, :] + scale * here
                else:
                    final_out[rows, :] = scale * here
                noise_out[step, rows, :] = here
    norm_rows(state, 2 * TOK, gain[...], normed, scaled1_out, spread1_out, 0)
    for part in range(6):
        packed1_out[:, part * 512 : (part + 1) * 512] = dot(
            normed[: 2 * TOK, :], w_qkv[:, part * 512 : (part + 1) * 512]
        ).astype(BF16)
    attend(2, packed1_out, weights1_out, mixed, lat1, 0)
    for part in range(4):
        at = slice(part * 256, (part + 1) * 256)
        branch = dot(mixed[: 2 * TOK, :], w_out[:, at])
        final = state[: 2 * TOK, at] + branch + final_out[:, at]
        final_out[:, at] = final
        sent_out[:, at] = final.astype(BF16)
    fill(ext, target, west[3].astype(F32), east[3].astype(F32))
    for row in range(LAT):
        part = frame(ext, row, origin1 + WIN, 16)
        for window in range(2):
            rows = slice(window * TOK + row * WIN, window * TOK + (row + 1) * WIN)
            target_out[rows, :] = part[window * WIN : (window + 1) * WIN]


def vmem():
    return pl.BlockSpec(memory_space=pltpu.VMEM)


def smem():
    return pl.BlockSpec(memory_space=pltpu.SMEM)


def anywhere():
    return pl.BlockSpec(memory_space=pl.ANY)


def forward(shifts, initial, target, noise, east, west, gain, noise_scale, w_qkv, w_out):
    rows = 2 * TOK
    saved = [
        jax.ShapeDtypeStruct((rows, 3 * C), BF16),
        jax.ShapeDtypeStruct((2 * GROUPS, TOK, SPAN), BF16),
        jax.ShapeDtypeStruct((rows, C), F32),
        jax.ShapeDtypeStruct((rows, 128), F32),
    ]
    out_shape = [
        jax.ShapeDtypeStruct((rows, C), F32),
        jax.ShapeDtypeStruct((rows, C), BF16),
        jax.ShapeDtypeStruct((rows, C), F32),
        jax.ShapeDtypeStruct((2, rows, C), F32),
    ] + saved * 2
    return pl.pallas_call(
        forward_kernel,
        out_shape=out_shape,
        in_specs=[smem()] + [vmem()] * 7 + [anywhere()] * 2,
        out_specs=[vmem()] * len(out_shape),
        scratch_shapes=[
            pltpu.VMEM((C, 3 * C), BF16),
            pltpu.VMEM((C, C), BF16),
            pltpu.VMEM((LAT, 32, C), F32),
            pltpu.VMEM((3 * TOK, C), F32),
            pltpu.VMEM((3 * TOK, C), BF16),
            pltpu.VMEM((3 * TOK, 3 * C), BF16),
            pltpu.VMEM((3 * TOK, C), BF16),
            pltpu.SemaphoreType.DMA((7,)),
        ],
        compiler_params=pltpu.CompilerParams(vmem_limit_bytes=VMEM_LIMIT),
        name="forward",
    )(shifts, initial, target, noise, east, west, gain, noise_scale, w_qkv, w_out)


def attend_back(packed, weights_ref, d_mixed, d_packed):
    masks = head_masks()

    def group(at, _):
        for window in range(2):
            rows = slice(window * TOK, (window + 1) * TOK)
            here = lanes(at * LANES, LANES)
            queries = packed[rows, here]
            keys = packed[rows, lanes(C + at * LANES, LANES)]
            values = packed[rows, lanes(2 * C + at * LANES, LANES)]
            d_mixed_blocks = by_head(d_mixed[rows, here], masks)
            weights = weights_ref[window * GROUPS + at]
            d_weights = dot_nt(values, d_mixed_blocks)
            d_values = dot(weights, d_mixed_blocks)
            probs = weights.astype(F32)
            centred = d_weights - jnp.sum(d_weights * probs, axis=0, keepdims=True)
            d_scores = (probs * centred * SCALE).astype(BF16)
            d_keys = dot(d_scores, by_head(queries, masks))
            d_queries = fold_heads(dot_tn(d_scores, keys), masks)
            d_packed[rows, here] = d_queries.astype(BF16)
            d_packed[rows, lanes(C + at * LANES, LANES)] = d_keys.astype(BF16)
            d_packed[rows, lanes(2 * C + at * LANES, LANES)] = d_values.astype(BF16)
        return 0

    lax.fori_loop(0, GROUPS, group, 0)


def slope(difference):
    return difference * lax.rsqrt(difference * difference + SMOOTH * SMOOTH)


def start_weights(w_qkv_hbm, w_out_hbm, w_qkv, w_out, sems):
    copies = [pltpu.make_async_copy(w_out_hbm, w_out, sems.at[4])]
    for part in range(4):
        at = pl.ds(part * 256, 256)
        copies.append(pltpu.make_async_copy(w_qkv_hbm.at[at], w_qkv.at[at], sems.at[part]))
    for copy in copies:
        copy.start()
    return copies


def step_back(
    copies, d_next, packed, weights, scaled, spread, gain, w_qkv, w_out, d_mixed, d_packed, d_normed
):
    copies[0].wait()
    d_branch = d_next[...].astype(BF16)
    for part in range(4):
        at = slice(part * 256, (part + 1) * 256)
        d_mixed[:, at] = dot_nt(d_branch, w_out[at, :]).astype(BF16)
    attend_back(packed, weights, d_mixed, d_packed)
    for part in range(4):
        at = slice(part * 256, (part + 1) * 256)
        copies[1 + part].wait()
        d_normed[:, at] = dot_nt(d_packed[...], w_qkv[at, :])


def norm_back(at, d_next, scaled_ref, spread_ref, d_normed, gain):
    rows = slice(at, at + 32)
    scaled = scaled_ref[rows, :]
    d_here = d_normed[rows, :]
    d_hat = d_here * gain
    spread = spread_ref[rows, 0:1]
    d_fields = spread * (
        d_hat
        - jnp.mean(d_hat, axis=-1, keepdims=True)
        - scaled * jnp.mean(d_hat * scaled, axis=-1, keepdims=True)
    )
    return d_next[rows, :] + d_fields, eight_rows(d_here * scaled)


def eight_rows(value):
    out = value[0:8]
    for at in range(8, value.shape[0], 8):
        out = out + value[at : at + 8]
    return out


def backward1_kernel(
    final,
    near,
    far,
    far_near,
    target,
    noise,
    packed,
    weights,
    scaled,
    spread,
    gain,
    w_qkv_hbm,
    w_out_hbm,
    d_out,
    head_out,
    gain_out,
    scale_out,
    w_qkv,
    w_out,
    d_next,
    d_mixed,
    d_packed,
    d_normed,
    sems,
):
    copies = start_weights(w_qkv_hbm, w_out_hbm, w_qkv, w_out, sems)
    scale_total = jnp.zeros((8, C), F32)
    for at in range(0, 2 * TOK, 32):
        rows = slice(at, at + 32)
        here = final[rows, :]
        pairs = (
            slope(here - near[rows, :].astype(F32))
            + slope(here - far[rows, :].astype(F32))
            + slope(here - far_near[rows, :].astype(F32))
        )
        seed = slope(here - target[rows, :]) - pairs * (1.0 / 3.0)
        d_next[rows, :] = seed
        scale_total = scale_total + eight_rows(seed * noise[1, rows, :])
    step_back(
        copies, d_next, packed, weights, scaled, spread, gain, w_qkv, w_out, d_mixed, d_packed, d_normed
    )
    gain_total = jnp.zeros((8, C), F32)
    for at in range(0, 2 * TOK, 32):
        rows = slice(at, at + 32)
        d_here, gain_part = norm_back(at, d_next, scaled, spread, d_normed, gain[...])
        d_out[rows, :] = d_here
        if at < TOK:
            head_out[rows, :] = d_here.astype(BF16)
        gain_total = gain_total + gain_part
        scale_total = scale_total + eight_rows(d_here * noise[0, rows, :])
    gain_out[...] = gain_total
    scale_out[...] = scale_total


def backward0_kernel(
    shifts,
    d_in,
    d_east,
    packed,
    weights,
    scaled,
    spread,
    gain,
    gain_in,
    scale_in,
    w_qkv_hbm,
    w_out_hbm,
    own_out,
    tail_out,
    sums_out,
    w_qkv,
    w_out,
    ext,
    d_next,
    d_mixed,
    d_packed,
    d_normed,
    sems,
):
    copies = start_weights(w_qkv_hbm, w_out_hbm, w_qkv, w_out, sems)
    lon0, lon1 = shifts[0, 1], shifts[1, 1]
    origin1 = jnp.where(lon1 <= lon0, lon1, lon1 - WIN)
    east = d_east[...].astype(F32)
    for row in range(LAT):
        ext[row, 0:8, :] = d_in[row * WIN : (row + 1) * WIN, :]
        ext[row, 8:16, :] = d_in[TOK + row * WIN : TOK + (row + 1) * WIN, :]
        ext[row, 16:24, :] = east[row * WIN : (row + 1) * WIN]
    for row in range(LAT):
        part = frame(ext, row, lon0 - origin1, 16)
        for window in range(2):
            rows = slice(window * TOK + row * WIN, window * TOK + (row + 1) * WIN)
            d_next[rows, :] = part[window * WIN : (window + 1) * WIN]
    step_back(
        copies, d_next, packed, weights, scaled, spread, gain, w_qkv, w_out, d_mixed, d_packed, d_normed
    )
    gain_total = gain_in[...]
    for at in range(0, 2 * TOK, 32):
        d_here, gain_part = norm_back(at, d_next, scaled, spread, d_normed, gain[...])
        gain_total = gain_total + gain_part
        for piece in range(4):
            token = at + piece * WIN
            row, window = (token % TOK) // WIN, token // TOK
            ext[row, 8 + window * WIN : 16 + window * WIN, :] = d_here[
                piece * WIN : (piece + 1) * WIN
            ]
    sums_out[0:1, :] = jnp.sum(gain_total, axis=0, keepdims=True)
    sums_out[1:2, :] = jnp.sum(scale_in[...], axis=0, keepdims=True)
    tails = []
    for row in range(LAT):
        own_out[row] = frame(ext, row, WIN - lon0, 16)
        tails.append(frame(ext, row, 24 - lon0, WIN))
    tail_out[...] = jnp.concatenate(tails, axis=0).astype(BF16)


def backward_scratch():
    rows = 2 * TOK
    return [
        pltpu.VMEM((rows, C), F32),
        pltpu.VMEM((rows, C), BF16),
        pltpu.VMEM((rows, 3 * C), BF16),
        pltpu.VMEM((rows, C), F32),
        pltpu.SemaphoreType.DMA((5,)),
    ]


def backward1(final, others, target, noise, saved, gain, w_qkv, w_out):
    rows = 2 * TOK
    return pl.pallas_call(
        backward1_kernel,
        out_shape=[
            jax.ShapeDtypeStruct((rows, C), F32),
            jax.ShapeDtypeStruct((TOK, C), BF16),
            jax.ShapeDtypeStruct((8, C), F32),
            jax.ShapeDtypeStruct((8, C), F32),
        ],
        in_specs=[vmem()] * 11 + [anywhere()] * 2,
        out_specs=[vmem()] * 4,
        scratch_shapes=[pltpu.VMEM((C, 3 * C), BF16), pltpu.VMEM((C, C), BF16)]
        + backward_scratch(),
        compiler_params=pltpu.CompilerParams(vmem_limit_bytes=VMEM_LIMIT),
        name="backward1",
    )(final, *others, target, noise, *saved, gain, w_qkv, w_out)


def backward0(shifts, d_in, d_east, saved, gain, gain_in, scale_in, w_qkv, w_out):
    return pl.pallas_call(
        backward0_kernel,
        out_shape=[
            jax.ShapeDtypeStruct((LAT, 16, C), F32),
            jax.ShapeDtypeStruct((TOK, C), BF16),
            jax.ShapeDtypeStruct((2, C), F32),
        ],
        in_specs=[smem()] + [vmem()] * 9 + [anywhere()] * 2,
        out_specs=[vmem()] * 3,
        scratch_shapes=[
            pltpu.VMEM((C, 3 * C), BF16),
            pltpu.VMEM((C, C), BF16),
            pltpu.VMEM((LAT, 32, C), F32),
        ]
        + backward_scratch(),
        compiler_params=pltpu.CompilerParams(vmem_limit_bytes=VMEM_LIMIT),
        name="backward0",
    )(shifts, d_in, d_east, *saved, gain, gain_in, scale_in, w_qkv, w_out)


def along(value, axis, steps):
    count = lax.axis_size(axis)
    return lax.ppermute(value, axis, [(at, (at + steps) % count) for at in range(count)])


def swapped(value, axis, bit):
    count = lax.axis_size(axis)
    return lax.ppermute(value, axis, [(at, at ^ bit) for at in range(count)])


def total_over_devices(value):
    for axis in ("member", "tile"):
        bit = 1
        while bit < lax.axis_size(axis):
            value = value + swapped(value, axis, bit)
            bit *= 2
    return value


def local(initial, target, noise, w_qkv, w_out, gain, noise_scale, shifts):
    initial, noise = initial[0], noise[:, 0]

    def border(at):
        parts = [
            part[:, at].reshape(TOK, C).astype(BF16)
            for part in (initial, noise[0], noise[1], target)
        ]
        return jnp.stack(parts)

    east = along(border(slice(0, WIN)), "tile", -1)
    west = along(border(slice(WIN, 2 * WIN)), "tile", 1)
    gain_row, scale_row = gain[None], noise_scale[None]
    final, sent, target_here, noise_here, *saved = forward(
        shifts, initial, target, noise, east, west, gain_row, scale_row, w_qkv, w_out
    )
    far = swapped(sent, "member", 2)
    near = swapped(sent, "member", 1)
    far_near = swapped(far, "member", 1)
    d_one, head, gain_part, scale_part = backward1(
        final, (near, far, far_near), target_here, noise_here, saved[4:], gain_row, w_qkv, w_out
    )
    own, tail, sums = backward0(
        shifts,
        d_one,
        along(head, "tile", -1),
        saved[:4],
        gain_row,
        gain_part,
        scale_part,
        w_qkv,
        w_out,
    )
    arrived = along(tail, "tile", 1).reshape(LAT, WIN, C).astype(F32)
    column = jnp.arange(WIN)[None, :, None]
    first = jnp.where(column < shifts[0, 1], arrived, own[:, :WIN])
    state_grad = jnp.concatenate([first, own[:, WIN:]], axis=1)[None]
    sums = total_over_devices(sums)
    members = lax.axis_size("member")
    factor = (members * LAT * initial.shape[1] * lax.axis_size("tile")) ** (-0.5)
    return (state_grad, sums[0] * factor, sums[1] * factor)


def solution(mesh):
    in_specs = (
        P("member", None, "tile", None),
        P(None, "tile", None),
        P(None, "member", None, "tile", None),
        P(),
        P(),
        P(),
        P(),
        P(),
    )
    out_specs = (P("member", None, "tile", None), P(), P())
    return jax.shard_map(local, mesh=mesh, in_specs=in_specs, out_specs=out_specs, check_vma=False)
```

```python
import functools

import jax
import jax.numpy as jnp
from jax import lax
from jax.experimental import pallas as pl
from jax.experimental.pallas import tpu as pltpu
from jax.sharding import PartitionSpec as P

C = 1024
HEAD = 32
WIN = 8
LAT = 8
TOK = LAT * WIN
GROUP = 4
LANES = GROUP * HEAD
GROUPS = C // LANES
SPAN = GROUP * TOK
SCALE = HEAD ** (-0.5)
SMOOTH = 0.25
F32 = jnp.float32
BF16 = jnp.bfloat16
VMEM_LIMIT = 16 * 1024 * 1024


def dot(left, right):
    return lax.dot_general(left, right, (((1,), (0,)), ((), ())), preferred_element_type=F32)


def dot_nt(left, right):
    return lax.dot_general(left, right, (((1,), (1,)), ((), ())), preferred_element_type=F32)


def dot_tn(left, right):
    return lax.dot_general(left, right, (((0,), (0,)), ((), ())), preferred_element_type=F32)


def head_masks():
    lane = lax.broadcasted_iota(jnp.int32, (TOK, LANES), 1) // HEAD
    return [lane == head for head in range(GROUP)]


def by_head(value, masks):
    zero = jnp.zeros_like(value)
    return jnp.concatenate([jnp.where(mask, value, zero) for mask in masks], axis=0)


def fold_heads(stacked, masks):
    out = stacked[:TOK]
    for head in range(1, GROUP):
        out = jnp.where(masks[head], stacked[head * TOK : (head + 1) * TOK], out)
    return out


def lat_mask(lat_shift):
    key_lat = lax.broadcasted_iota(jnp.int32, (TOK, SPAN), 0) // WIN
    query_lat = (lax.broadcasted_iota(jnp.int32, (TOK, SPAN), 1) % TOK) // WIN
    return (key_lat < lat_shift) == (query_lat < lat_shift)


def lanes(start, size):
    return pl.ds(pl.multiple_of(start, 128), size)


def fill(ext, own_ref, west, east):
    for row in range(LAT):
        ext[row, 0:8, :] = west[row * WIN : (row + 1) * WIN]
        ext[row, 8:24, :] = own_ref[row].astype(F32)
        ext[row, 24:32, :] = east[row * WIN : (row + 1) * WIN]


def frame(ext, row, start, columns):
    held = ext.shape[1]
    return pltpu.roll(ext[row], lax.rem(held - start, held), 0)[:columns]


def norm_rows(x_ref, rows, gain, normed_ref, scaled_ref, spread_ref, saved_from):
    for at in range(0, rows, 32):
        x = x_ref[at : at + 32, :]
        centre = jnp.mean(x, axis=-1, keepdims=True)
        offset = x - centre
        spread = lax.rsqrt(jnp.mean(offset * offset, axis=-1, keepdims=True) + 1e-05)
        scaled = offset * spread
        normed_ref[at : at + 32, :] = (scaled * gain).astype(BF16)
        if at >= saved_from:
            scaled_ref[at - saved_from : at - saved_from + 32, :] = scaled
            spread_ref[at - saved_from : at - saved_from + 32, :] = jnp.broadcast_to(
                spread, (32, 128)
            )


def attend(windows, packed_ref, weights_ref, mixed_ref, lat_shift, saved_from):
    masks = head_masks()
    allowed = lat_mask(lat_shift)

    def group(at, _):
        for window in range(windows):
            rows = slice(window * TOK, (window + 1) * TOK)
            queries = packed_ref[rows, lanes(at * LANES, LANES)]
            keys = packed_ref[rows, lanes(C + at * LANES, LANES)]
            values = packed_ref[rows, lanes(2 * C + at * LANES, LANES)]
            scores = dot_nt(keys, by_head(queries, masks))
            scores = jnp.where(allowed, scores, -1e9 / SCALE)
            highest = jnp.max(scores, axis=0, keepdims=True)
            raised = jnp.exp((scores - highest) * SCALE)
            total = jnp.sum(raised, axis=0, keepdims=True)
            weights = (raised * (1.0 / total)).astype(BF16)
            if window >= saved_from:
                weights_ref[(window - saved_from) * GROUPS + at] = weights
            mixed = fold_heads(dot_tn(weights, values), masks)
            mixed_ref[rows, lanes(at * LANES, LANES)] = mixed.astype(BF16)
        return 0

    lax.fori_loop(0, GROUPS, group, 0, unroll=GROUPS)


def window_rows(window, row):
    start = window * TOK + row * WIN
    return slice(start, start + WIN)


def forward0_kernel(
    shifts,
    initial,
    east,
    west,
    gain,
    w_qkv,
    w_out,
    following_out,
    packed_out,
    weights_out,
    scaled_out,
    spread_out,
    ext,
    state,
    normed,
    packed,
    mixed,
):
    lat_shift, lon_shift = shifts[0, 0], shifts[0, 1]
    fill(ext, initial, west[...].astype(F32), east[...].astype(F32))
    for row in range(LAT):
        part = frame(ext, row, lon_shift, 24)
        for window in range(3):
            state[window_rows(window, row), :] = part[window * WIN : (window + 1) * WIN]
    norm_rows(state, 3 * TOK, gain[...], normed, scaled_out, spread_out, TOK)
    for part in range(6):
        at = slice(part * 512, (part + 1) * 512)
        packed[:, at] = dot(normed[...], w_qkv[:, at]).astype(BF16)
    packed_out[...] = packed[TOK:, :]
    attend(3, packed, weights_out, mixed, lat_shift, 1)
    for part in range(4):
        at = slice(part * 256, (part + 1) * 256)
        following = state[:, at] + dot(mixed[...], w_out[:, at])
        for row in range(LAT):
            for window in range(3):
                following_out[row, window * WIN : (window + 1) * WIN, at] = following[
                    window_rows(window, row)
                ]


def forward1_kernel(
    shifts,
    before,
    noise,
    east,
    west,
    gain,
    noise_scale,
    w_qkv,
    w_out,
    final_out,
    sent_out,
    noise_out,
    packed_out,
    weights_out,
    scaled_out,
    spread_out,
    ext,
    state,
    normed,
    mixed,
):
    lat_shift = shifts[1, 0]
    lon0, origin1 = shifts[0, 1], origin(shifts)
    scale = noise_scale[...]
    for step in range(2):
        fill(ext, noise.at[step], west[step].astype(F32), east[step].astype(F32))
        for row in range(LAT):
            part = frame(ext, row, origin1 + WIN, 16)
            fields = frame(before, row, origin1 - lon0 + WIN, 16)
            for window in range(2):
                rows = window_rows(window, row)
                here = part[window * WIN : (window + 1) * WIN]
                if step == 0:
                    state[rows, :] = fields[window * WIN : (window + 1) * WIN] + scale * here
                else:
                    final_out[rows, :] = state[rows, :] + scale * here
                noise_out[step, rows, :] = here
    norm_rows(state, 2 * TOK, gain[...], normed, scaled_out, spread_out, 0)
    for part in range(6):
        at = slice(part * 512, (part + 1) * 512)
        packed_out[:, at] = dot(normed[...], w_qkv[:, at]).astype(BF16)
    attend(2, packed_out, weights_out, mixed, lat_shift, 0)
    for part in range(4):
        at = slice(part * 256, (part + 1) * 256)
        final = final_out[:, at] + dot(mixed[...], w_out[:, at])
        final_out[:, at] = final
        sent_out[:, at] = final.astype(BF16)


def origin(shifts):
    lon0, lon1 = shifts[0, 1], shifts[1, 1]
    return jnp.where(lon1 <= lon0, lon1, lon1 - WIN)


def vmem():
    return pl.BlockSpec(memory_space=pltpu.VMEM)


def smem():
    return pl.BlockSpec(memory_space=pltpu.SMEM)


def compiler_params():
    return pltpu.CompilerParams(vmem_limit_bytes=VMEM_LIMIT)


def saved_shapes():
    rows = 2 * TOK
    return [
        jax.ShapeDtypeStruct((rows, 3 * C), BF16),
        jax.ShapeDtypeStruct((2 * GROUPS, TOK, SPAN), BF16),
        jax.ShapeDtypeStruct((rows, C), F32),
        jax.ShapeDtypeStruct((rows, 128), F32),
    ]


def forward0(shifts, initial, east, west, gain, w_qkv, w_out):
    rows = 3 * TOK
    out_shape = [jax.ShapeDtypeStruct((LAT, 24, C), F32)] + saved_shapes()
    return pl.pallas_call(
        forward0_kernel,
        out_shape=out_shape,
        in_specs=[smem()] + [vmem()] * 6,
        out_specs=[vmem()] * len(out_shape),
        scratch_shapes=[
            pltpu.VMEM((LAT, 32, C), F32),
            pltpu.VMEM((rows, C), F32),
            pltpu.VMEM((rows, C), BF16),
            pltpu.VMEM((rows, 3 * C), BF16),
            pltpu.VMEM((rows, C), BF16),
        ],
        compiler_params=compiler_params(),
        name="forward0",
    )(shifts, initial, east, west, gain, w_qkv, w_out)


def forward1(shifts, before, noise, east, west, gain, noise_scale, w_qkv, w_out):
    rows = 2 * TOK
    out_shape = [
        jax.ShapeDtypeStruct((rows, C), F32),
        jax.ShapeDtypeStruct((rows, C), BF16),
        jax.ShapeDtypeStruct((2, rows, C), F32),
    ] + saved_shapes()
    return pl.pallas_call(
        forward1_kernel,
        out_shape=out_shape,
        in_specs=[smem()] + [vmem()] * 8,
        out_specs=[vmem()] * len(out_shape),
        scratch_shapes=[
            pltpu.VMEM((LAT, 32, C), F32),
            pltpu.VMEM((rows, C), F32),
            pltpu.VMEM((rows, C), BF16),
            pltpu.VMEM((rows, C), BF16),
        ],
        compiler_params=compiler_params(),
        name="forward1",
    )(shifts, before, noise, east, west, gain, noise_scale, w_qkv, w_out)


def attend_back(packed, weights_ref, d_mixed, d_packed):
    masks = head_masks()

    def group(at, _):
        for window in range(2):
            rows = slice(window * TOK, (window + 1) * TOK)
            here = lanes(at * LANES, LANES)
            queries = packed[rows, here]
            keys = packed[rows, lanes(C + at * LANES, LANES)]
            values = packed[rows, lanes(2 * C + at * LANES, LANES)]
            d_mixed_blocks = by_head(d_mixed[rows, here], masks)
            weights = weights_ref[window * GROUPS + at]
            d_weights = dot_nt(values, d_mixed_blocks)
            d_values = dot(weights, d_mixed_blocks)
            probs = weights.astype(F32)
            centred = d_weights - jnp.sum(d_weights * probs, axis=0, keepdims=True)
            d_scores = (probs * centred * SCALE).astype(BF16)
            d_keys = dot(d_scores, by_head(queries, masks))
            d_queries = fold_heads(dot_tn(d_scores, keys), masks)
            d_packed[rows, here] = d_queries.astype(BF16)
            d_packed[rows, lanes(C + at * LANES, LANES)] = d_keys.astype(BF16)
            d_packed[rows, lanes(2 * C + at * LANES, LANES)] = d_values.astype(BF16)
        return 0

    lax.fori_loop(0, GROUPS, group, 0, unroll=GROUPS)


def slope(difference):
    return difference * lax.rsqrt(difference * difference + SMOOTH * SMOOTH)


def step_back(
    d_next, packed, weights, w_qkv_t, w_out_t, d_mixed, d_packed, d_normed
):
    d_branch = d_next[...].astype(BF16)
    for part in range(4):
        at = slice(part * 256, (part + 1) * 256)
        d_mixed[:, at] = dot(d_branch, w_out_t[:, at]).astype(BF16)
    attend_back(packed, weights, d_mixed, d_packed)
    for part in range(4):
        at = slice(part * 256, (part + 1) * 256)
        d_normed[:, at] = dot(d_packed[...], w_qkv_t[:, at])


def norm_back(at, d_next, scaled_ref, spread_ref, d_normed, gain):
    rows = slice(at, at + 32)
    scaled = scaled_ref[rows, :]
    d_here = d_normed[rows, :]
    d_hat = d_here * gain
    spread = spread_ref[rows, 0:1]
    d_fields = spread * (
        d_hat
        - jnp.mean(d_hat, axis=-1, keepdims=True)
        - scaled * jnp.mean(d_hat * scaled, axis=-1, keepdims=True)
    )
    return d_next[rows, :] + d_fields, eight_rows(d_here * scaled)


def eight_rows(value):
    out = value[0:8]
    for at in range(8, value.shape[0], 8):
        out = out + value[at : at + 8]
    return out


def backward1_kernel(
    shifts,
    final,
    near,
    far,
    far_near,
    target,
    east,
    west,
    noise,
    packed,
    weights,
    scaled,
    spread,
    gain,
    w_qkv_t,
    w_out_t,
    d_out,
    head_out,
    gain_out,
    scale_out,
    ext,
    d_next,
    d_mixed,
    d_packed,
    d_normed,
):
    fill(ext, target, west[...].astype(F32), east[...].astype(F32))
    for row in range(LAT):
        part = frame(ext, row, origin(shifts) + WIN, 16)
        for window in range(2):
            d_normed[window_rows(window, row), :] = part[window * WIN : (window + 1) * WIN]
    scale_total = jnp.zeros((8, C), F32)
    for at in range(0, 2 * TOK, 32):
        rows = slice(at, at + 32)
        here = final[rows, :]
        pairs = (
            slope(here - near[rows, :].astype(F32))
            + slope(here - far[rows, :].astype(F32))
            + slope(here - far_near[rows, :].astype(F32))
        )
        seed = slope(here - d_normed[rows, :]) - pairs * (1.0 / 3.0)
        d_next[rows, :] = seed
        scale_total = scale_total + eight_rows(seed * noise[1, rows, :])
    step_back(d_next, packed, weights, w_qkv_t, w_out_t, d_mixed, d_packed, d_normed)
    gain_total = jnp.zeros((8, C), F32)
    for at in range(0, 2 * TOK, 32):
        rows = slice(at, at + 32)
        d_here, gain_part = norm_back(at, d_next, scaled, spread, d_normed, gain[...])
        d_out[rows, :] = d_here
        if at < TOK:
            head_out[rows, :] = d_here.astype(BF16)
        gain_total = gain_total + gain_part
        scale_total = scale_total + eight_rows(d_here * noise[0, rows, :])
    gain_out[...] = gain_total
    scale_out[...] = scale_total


def backward0_kernel(
    shifts,
    d_in,
    d_east,
    packed,
    weights,
    scaled,
    spread,
    gain,
    gain_in,
    scale_in,
    w_qkv_t,
    w_out_t,
    own_out,
    tail_out,
    sums_out,
    ext,
    d_next,
    d_mixed,
    d_packed,
    d_normed,
):
    lon0, origin1 = shifts[0, 1], origin(shifts)
    east = d_east[...].astype(F32)
    for row in range(LAT):
        ext[row, 0:8, :] = d_in[row * WIN : (row + 1) * WIN, :]
        ext[row, 8:16, :] = d_in[TOK + row * WIN : TOK + (row + 1) * WIN, :]
        ext[row, 16:24, :] = east[row * WIN : (row + 1) * WIN]
    for row in range(LAT):
        part = frame(ext, row, lon0 - origin1, 16)
        for window in range(2):
            d_next[window_rows(window, row), :] = part[window * WIN : (window + 1) * WIN]
    step_back(d_next, packed, weights, w_qkv_t, w_out_t, d_mixed, d_packed, d_normed)
    gain_total = gain_in[...]
    for at in range(0, 2 * TOK, 32):
        d_here, gain_part = norm_back(at, d_next, scaled, spread, d_normed, gain[...])
        gain_total = gain_total + gain_part
        for piece in range(4):
            token = at + piece * WIN
            row, window = (token % TOK) // WIN, token // TOK
            ext[row, 8 + window * WIN : 16 + window * WIN, :] = d_here[
                piece * WIN : (piece + 1) * WIN
            ]
    sums_out[0:1, :] = jnp.sum(gain_total, axis=0, keepdims=True)
    sums_out[1:2, :] = jnp.sum(scale_in[...], axis=0, keepdims=True)
    tails = []
    for row in range(LAT):
        own_out[row] = frame(ext, row, WIN - lon0, 16)
        tails.append(frame(ext, row, 24 - lon0, WIN))
    tail_out[...] = jnp.concatenate(tails, axis=0).astype(BF16)


def backward_scratch():
    rows = 2 * TOK
    return [
        pltpu.VMEM((LAT, 32, C), F32),
        pltpu.VMEM((rows, C), F32),
        pltpu.VMEM((rows, C), BF16),
        pltpu.VMEM((rows, 3 * C), BF16),
        pltpu.VMEM((rows, C), F32),
    ]


def backward1(shifts, final, others, target, east, west, noise, saved, gain, w_qkv_t, w_out_t):
    rows = 2 * TOK
    return pl.pallas_call(
        backward1_kernel,
        out_shape=[
            jax.ShapeDtypeStruct((rows, C), F32),
            jax.ShapeDtypeStruct((TOK, C), BF16),
            jax.ShapeDtypeStruct((8, C), F32),
            jax.ShapeDtypeStruct((8, C), F32),
        ],
        in_specs=[smem()] + [vmem()] * 15,
        out_specs=[vmem()] * 4,
        scratch_shapes=backward_scratch(),
        compiler_params=compiler_params(),
        name="backward1",
    )(shifts, final, *others, target, east, west, noise, *saved, gain, w_qkv_t, w_out_t)


def backward0(shifts, d_in, d_east, saved, gain, gain_in, scale_in, w_qkv_t, w_out_t):
    return pl.pallas_call(
        backward0_kernel,
        out_shape=[
            jax.ShapeDtypeStruct((LAT, 16, C), F32),
            jax.ShapeDtypeStruct((TOK, C), BF16),
            jax.ShapeDtypeStruct((2, C), F32),
        ],
        in_specs=[smem()] + [vmem()] * 11,
        out_specs=[vmem()] * 3,
        scratch_shapes=backward_scratch(),
        compiler_params=compiler_params(),
        name="backward0",
    )(shifts, d_in, d_east, *saved, gain, gain_in, scale_in, w_qkv_t, w_out_t)


def along(value, axis, steps):
    count = lax.axis_size(axis)
    return lax.ppermute(value, axis, [(at, (at + steps) % count) for at in range(count)])


def swapped(value, axis, bit):
    count = lax.axis_size(axis)
    return lax.ppermute(value, axis, [(at, at ^ bit) for at in range(count)])


def total_over_devices(value, axis):
    bit = 1
    while bit < lax.axis_size(axis):
        value = value + swapped(value, axis, bit)
        bit *= 2
    return value


def local(initial, target, noise, w_qkv, w_out, gain, noise_scale, shifts):
    initial, noise = initial[0], noise[:, 0]

    def both_ways(part):
        shape = part.shape[:-3] + (TOK, C)
        first = part[..., :WIN, :].reshape(shape).astype(BF16)
        last = part[..., WIN:, :].reshape(shape).astype(BF16)
        return along(first, "tile", -1), along(last, "tile", 1)

    initial_sides = both_ways(initial)
    noise_sides = both_ways(noise)
    target_sides = both_ways(target)
    w_qkv_t, w_out_t = w_qkv.T, w_out.T
    gain_row, scale_row = gain[None], noise_scale[None]
    before, *saved0 = forward0(shifts, initial, *initial_sides, gain_row, w_qkv, w_out)
    final, sent, noise_here, *saved1 = forward1(
        shifts, before, noise, *noise_sides, gain_row, scale_row, w_qkv, w_out
    )
    far = swapped(sent, "member", 2)
    near = swapped(sent, "member", 1)
    far_near = swapped(far, "member", 1)
    d_one, head, gain_part, scale_part = backward1(
        shifts,
        final,
        (near, far, far_near),
        target,
        *target_sides,
        noise_here,
        saved1,
        gain_row,
        w_qkv_t,
        w_out_t,
    )
    own, tail, sums = backward0(
        shifts,
        d_one,
        along(head, "tile", -1),
        saved0,
        gain_row,
        gain_part,
        scale_part,
        w_qkv_t,
        w_out_t,
    )
    arrived = along(tail, "tile", 1)
    sums = total_over_devices(sums, "member")
    sums, arrived = lax.optimization_barrier((sums, arrived))
    column = jnp.arange(WIN)[None, :, None]
    first = jnp.where(
        column < shifts[0, 1], arrived.reshape(LAT, WIN, C).astype(F32), own[:, :WIN]
    )
    state_grad = jnp.concatenate([first, own[:, WIN:]], axis=1)[None]
    sums = total_over_devices(sums, "tile")
    members = lax.axis_size("member")
    factor = (members * LAT * initial.shape[1] * lax.axis_size("tile")) ** (-0.5)
    return (state_grad, sums[0] * factor, sums[1] * factor)


def solution(mesh):
    in_specs = (
        P("member", None, "tile", None),
        P(None, "tile", None),
        P(None, "member", None, "tile", None),
        P(),
        P(),
        P(),
        P(),
        P(),
    )
    out_specs = (P("member", None, "tile", None), P(), P())
    return jax.shard_map(local, mesh=mesh, in_specs=in_specs, out_specs=out_specs, check_vma=False)
```

```python
import functools

import jax
import jax.numpy as jnp
from jax import lax
from jax.experimental import pallas as pl
from jax.experimental.pallas import tpu as pltpu
from jax.sharding import PartitionSpec as P

C = 1024
HEAD = 32
WIN = 8
LAT = 8
TOK = LAT * WIN
GROUP = 4
LANES = GROUP * HEAD
GROUPS = C // LANES
SPAN = GROUP * TOK
SCALE = HEAD ** (-0.5)
SMOOTH = 0.25
F32 = jnp.float32
BF16 = jnp.bfloat16
VMEM_LIMIT = 28 * 1024 * 1024


def dot(left, right):
    return lax.dot_general(left, right, (((1,), (0,)), ((), ())), preferred_element_type=F32)


def dot_nt(left, right):
    return lax.dot_general(left, right, (((1,), (1,)), ((), ())), preferred_element_type=F32)


def dot_tn(left, right):
    return lax.dot_general(left, right, (((0,), (0,)), ((), ())), preferred_element_type=F32)


def head_masks():
    lane = lax.broadcasted_iota(jnp.int32, (TOK, LANES), 1) // HEAD
    return [lane == head for head in range(GROUP)]


def by_head(value, masks):
    zero = jnp.zeros_like(value)
    return jnp.concatenate([jnp.where(mask, value, zero) for mask in masks], axis=0)


def fold_heads(stacked, masks):
    out = stacked[:TOK]
    for head in range(1, GROUP):
        out = jnp.where(masks[head], stacked[head * TOK : (head + 1) * TOK], out)
    return out


def lat_mask(lat_shift):
    key_lat = lax.broadcasted_iota(jnp.int32, (TOK, SPAN), 0) // WIN
    query_lat = (lax.broadcasted_iota(jnp.int32, (TOK, SPAN), 1) % TOK) // WIN
    return (key_lat < lat_shift) == (query_lat < lat_shift)


def lanes(start, size):
    return pl.ds(pl.multiple_of(start, 128), size)


def fill(ext, own_ref, west, east):
    for row in range(LAT):
        ext[row, 0:8, :] = west[row * WIN : (row + 1) * WIN]
        ext[row, 8:24, :] = own_ref[row].astype(F32)
        ext[row, 24:32, :] = east[row * WIN : (row + 1) * WIN]


def frame(ext, row, start, columns):
    held = ext.shape[1]
    return pltpu.roll(ext[row], lax.rem(held - start, held), 0)[:columns]


def norm_rows(x_ref, rows, gain, normed_ref, scaled_ref, spread_ref, saved_from):
    for at in range(0, rows, 32):
        x = x_ref[at : at + 32, :]
        centre = jnp.mean(x, axis=-1, keepdims=True)
        offset = x - centre
        spread = lax.rsqrt(jnp.mean(offset * offset, axis=-1, keepdims=True) + 1e-05)
        scaled = offset * spread
        normed_ref[at : at + 32, :] = (scaled * gain).astype(BF16)
        if at >= saved_from:
            scaled_ref[at - saved_from : at - saved_from + 32, :] = scaled.astype(BF16)
            spread_ref[at - saved_from : at - saved_from + 32, :] = jnp.broadcast_to(
                spread, (32, 128)
            )


def attend(windows, packed_ref, weights_ref, mixed_ref, lat_shift, saved_from):
    masks = head_masks()
    allowed = lat_mask(lat_shift)

    def group(at, _):
        for window in range(windows):
            rows = slice(window * TOK, (window + 1) * TOK)
            queries = packed_ref[rows, lanes(at * LANES, LANES)]
            keys = packed_ref[rows, lanes(C + at * LANES, LANES)]
            values = packed_ref[rows, lanes(2 * C + at * LANES, LANES)]
            scores = dot_nt(keys, by_head(queries, masks))
            scores = jnp.where(allowed, scores, -1e9 / SCALE)
            highest = jnp.max(scores, axis=0, keepdims=True)
            raised = jnp.exp((scores - highest) * SCALE)
            total = jnp.sum(raised, axis=0, keepdims=True)
            weights = (raised * (1.0 / total)).astype(BF16)
            if window >= saved_from:
                weights_ref[(window - saved_from) * GROUPS + at] = weights
            mixed = fold_heads(dot_tn(weights, values), masks)
            mixed_ref[rows, lanes(at * LANES, LANES)] = mixed.astype(BF16)
        return 0

    lax.fori_loop(0, GROUPS, group, 0, unroll=GROUPS)


def window_rows(window, row):
    start = window * TOK + row * WIN
    return slice(start, start + WIN)


def start_copies(sems, first, pairs):
    copies = []
    for at, (source, destination) in enumerate(pairs):
        copy = pltpu.make_async_copy(source, destination, sems.at[first + at])
        copy.start()
        copies.append(copy)
    return copies


def wait_all(copies):
    for copy in copies:
        copy.wait()


def column_parts(source, destination, parts):
    width = source.shape[1] // parts
    return [
        (source.at[:, pl.ds(at * width, width)], destination.at[:, pl.ds(at * width, width)])
        for at in range(parts)
    ]


def forward0_kernel(
    initial_hbm,
    shifts_hbm,
    gain_hbm,
    w_qkv_hbm,
    w_out_hbm,
    east,
    west,
    following_out,
    packed_hbm,
    weights_hbm,
    scaled_hbm,
    spread_hbm,
    initial,
    shifts,
    gain,
    w_qkv,
    w_out,
    ext,
    state,
    normed,
    packed,
    mixed,
    weights,
    scaled,
    spread,
    sems,
):
    small = start_copies(
        sems, 0, [(shifts_hbm, shifts), (initial_hbm, initial), (gain_hbm, gain)]
    )
    parts = start_copies(sems, 3, column_parts(w_qkv_hbm, w_qkv, 6))
    late = start_copies(sems, 9, [(w_out_hbm, w_out)])
    wait_all(small)
    lat_shift, lon_shift = shifts[0, 0], shifts[0, 1]
    fill(ext, initial, west[...].astype(F32), east[...].astype(F32))
    for row in range(LAT):
        part = frame(ext, row, lon_shift, 24)
        for window in range(3):
            state[window_rows(window, row), :] = part[window * WIN : (window + 1) * WIN]
    norm_rows(state, 3 * TOK, gain[...], normed, scaled, spread, TOK)
    saves = start_copies(sems, 10, [(scaled, scaled_hbm), (spread, spread_hbm)])
    for part in range(6):
        at = slice(part * 512, (part + 1) * 512)
        parts[part].wait()
        packed[:, at] = dot(normed[...], w_qkv[:, at]).astype(BF16)
    saves += start_copies(sems, 12, [(packed.at[pl.ds(TOK, 2 * TOK)], packed_hbm)])
    attend(3, packed, weights, mixed, lat_shift, 1)
    saves += start_copies(sems, 13, [(weights, weights_hbm)])
    wait_all(late)
    for part in range(4):
        at = slice(part * 256, (part + 1) * 256)
        following = state[:, at] + dot(mixed[...], w_out[:, at])
        for row in range(LAT):
            for window in range(3):
                following_out[row, window * WIN : (window + 1) * WIN, at] = following[
                    window_rows(window, row)
                ]
    wait_all(saves)


def forward1_kernel(
    noise_hbm,
    shifts_hbm,
    gain_hbm,
    scale_hbm,
    w_qkv_hbm,
    w_out_hbm,
    before,
    east,
    west,
    sent_out,
    final_hbm,
    noise_out_hbm,
    packed_hbm,
    weights_hbm,
    scaled_hbm,
    spread_hbm,
    noise,
    shifts,
    gain,
    noise_scale,
    w_qkv,
    w_out,
    ext,
    state,
    final,
    noise_here,
    normed,
    packed,
    mixed,
    weights,
    scaled,
    spread,
    sems,
):
    small = start_copies(
        sems,
        0,
        [(shifts_hbm, shifts), (noise_hbm, noise), (gain_hbm, gain), (scale_hbm, noise_scale)],
    )
    parts = start_copies(sems, 4, column_parts(w_qkv_hbm, w_qkv, 6))
    late = start_copies(sems, 10, [(w_out_hbm, w_out)])
    wait_all(small)
    lat_shift = shifts[1, 0]
    lon0, origin1 = shifts[0, 1], origin(shifts)
    scale = noise_scale[...]
    for step in range(2):
        fill(ext, noise.at[step], west[step].astype(F32), east[step].astype(F32))
        for row in range(LAT):
            part = frame(ext, row, origin1 + WIN, 16)
            if step == 0:
                fields = frame(before, row, origin1 - lon0 + WIN, 16)
            for window in range(2):
                rows = window_rows(window, row)
                here = part[window * WIN : (window + 1) * WIN]
                if step == 0:
                    state[rows, :] = fields[window * WIN : (window + 1) * WIN] + scale * here
                else:
                    final[rows, :] = state[rows, :] + scale * here
                noise_here[step, rows, :] = here
    saves = start_copies(sems, 11, [(noise_here, noise_out_hbm)])
    norm_rows(state, 2 * TOK, gain[...], normed, scaled, spread, 0)
    saves += start_copies(sems, 12, [(scaled, scaled_hbm), (spread, spread_hbm)])
    for part in range(6):
        at = slice(part * 512, (part + 1) * 512)
        parts[part].wait()
        packed[:, at] = dot(normed[...], w_qkv[:, at]).astype(BF16)
    saves += start_copies(sems, 14, [(packed, packed_hbm)])
    attend(2, packed, weights, mixed, lat_shift, 0)
    saves += start_copies(sems, 15, [(weights, weights_hbm)])
    wait_all(late)
    for part in range(4):
        at = slice(part * 256, (part + 1) * 256)
        last = final[:, at] + dot(mixed[...], w_out[:, at])
        final[:, at] = last
        sent_out[:, at] = last.astype(BF16)
    saves += start_copies(sems, 16, [(final, final_hbm)])
    wait_all(saves)


def origin(shifts):
    lon0, lon1 = shifts[0, 1], shifts[1, 1]
    return jnp.where(lon1 <= lon0, lon1, lon1 - WIN)


def vmem():
    return pl.BlockSpec(memory_space=pltpu.VMEM)


def hbm():
    return pl.BlockSpec(memory_space=pltpu.HBM)


def compiler_params():
    return pltpu.CompilerParams(vmem_limit_bytes=VMEM_LIMIT)


ROWS = 2 * TOK
SAVED = [
    ((ROWS, 3 * C), BF16),
    ((2 * GROUPS, TOK, SPAN), BF16),
    ((ROWS, C), BF16),
    ((ROWS, 128), F32),
]


def shapes(entries):
    return [jax.ShapeDtypeStruct(shape, dtype) for shape, dtype in entries]


def buffers(entries):
    return [pltpu.VMEM(shape, dtype) for shape, dtype in entries]


WEIGHTS = [((C, 3 * C), BF16), ((C, C), BF16)]


def forward0(shifts, initial, east, west, gain, w_qkv, w_out):
    rows = 3 * TOK
    return pl.pallas_call(
        forward0_kernel,
        out_shape=shapes([((LAT, 24, C), F32)] + SAVED),
        in_specs=[hbm()] * 5 + [vmem()] * 2,
        out_specs=[vmem()] + [hbm()] * 4,
        scratch_shapes=[
            pltpu.VMEM((LAT, 16, C), F32),
            pltpu.SMEM((2, 2), jnp.int32),
            pltpu.VMEM((1, C), F32),
        ]
        + buffers(WEIGHTS)
        + buffers(
            [
                ((LAT, 32, C), F32),
                ((rows, C), F32),
                ((rows, C), BF16),
                ((rows, 3 * C), BF16),
                ((rows, C), BF16),
            ]
        )
        + buffers(SAVED[1:])
        + [pltpu.SemaphoreType.DMA((14,))],
        compiler_params=compiler_params(),
        name="forward0",
    )(initial, shifts, gain, w_qkv, w_out, east, west)


def forward1(shifts, before, noise, east, west, gain, noise_scale, w_qkv, w_out):
    return pl.pallas_call(
        forward1_kernel,
        out_shape=shapes([((ROWS, C), BF16), ((ROWS, C), F32), ((2, ROWS, C), F32)] + SAVED),
        in_specs=[hbm()] * 6 + [vmem()] * 3,
        out_specs=[vmem()] + [hbm()] * 6,
        scratch_shapes=[
            pltpu.VMEM((2, LAT, 16, C), BF16),
            pltpu.SMEM((2, 2), jnp.int32),
            pltpu.VMEM((1, C), F32),
            pltpu.VMEM((1, C), F32),
        ]
        + buffers(WEIGHTS)
        + buffers(
            [
                ((LAT, 32, C), F32),
                ((ROWS, C), F32),
                ((ROWS, C), F32),
                ((2, ROWS, C), F32),
                ((ROWS, C), BF16),
                ((ROWS, 3 * C), BF16),
                ((ROWS, C), BF16),
            ]
        )
        + buffers(SAVED[1:])
        + [pltpu.SemaphoreType.DMA((17,))],
        compiler_params=compiler_params(),
        name="forward1",
    )(noise, shifts, gain, noise_scale, w_qkv, w_out, before, east, west)


def transpose_kernel(source, out):
    out[...] = source[...].T


def transposed(matrix):
    columns = matrix.shape[1]
    return pl.pallas_call(
        transpose_kernel,
        grid=(columns // 256,),
        out_shape=jax.ShapeDtypeStruct((columns, C), BF16),
        in_specs=[pl.BlockSpec((C, 256), lambda at: (0, at))],
        out_specs=pl.BlockSpec((256, C), lambda at: (at, 0)),
        compiler_params=compiler_params(),
        name="transposed",
    )(matrix)


def attend_back(packed, weights_ref, d_mixed, d_packed):
    masks = head_masks()

    def group(at, _):
        for window in range(2):
            rows = slice(window * TOK, (window + 1) * TOK)
            here = lanes(at * LANES, LANES)
            queries = packed[rows, here]
            keys = packed[rows, lanes(C + at * LANES, LANES)]
            values = packed[rows, lanes(2 * C + at * LANES, LANES)]
            d_mixed_blocks = by_head(d_mixed[rows, here], masks)
            weights = weights_ref[window * GROUPS + at]
            d_weights = dot_nt(values, d_mixed_blocks)
            d_values = dot(weights, d_mixed_blocks)
            probs = weights.astype(F32)
            centred = d_weights - jnp.sum(d_weights * probs, axis=0, keepdims=True)
            d_scores = (probs * centred * SCALE).astype(BF16)
            d_keys = dot(d_scores, by_head(queries, masks))
            d_queries = fold_heads(dot_tn(d_scores, keys), masks)
            d_packed[rows, here] = d_queries.astype(BF16)
            d_packed[rows, lanes(C + at * LANES, LANES)] = d_keys.astype(BF16)
            d_packed[rows, lanes(2 * C + at * LANES, LANES)] = d_values.astype(BF16)
        return 0

    lax.fori_loop(0, GROUPS, group, 0, unroll=GROUPS)


def slope(difference):
    return difference * lax.rsqrt(difference * difference + SMOOTH * SMOOTH)


def step_back(
    copies, d_next, packed, weights, w_qkv_t, w_out_t, d_mixed, d_packed, d_normed
):
    out_t, packed_copy, weights_copy, *qkv_t = copies
    out_t.wait()
    d_branch = d_next[...].astype(BF16)
    for part in range(4):
        at = slice(part * 256, (part + 1) * 256)
        d_mixed[:, at] = dot(d_branch, w_out_t[:, at]).astype(BF16)
    packed_copy.wait()
    weights_copy.wait()
    attend_back(packed, weights, d_mixed, d_packed)
    for part in range(4):
        at = slice(part * 256, (part + 1) * 256)
        qkv_t[part].wait()
        d_normed[:, at] = dot(d_packed[...], w_qkv_t[:, at])


def norm_back(at, d_next, scaled_ref, spread_ref, d_normed, gain):
    rows = slice(at, at + 32)
    scaled = scaled_ref[rows, :].astype(F32)
    d_here = d_normed[rows, :]
    d_hat = d_here * gain
    spread = spread_ref[rows, 0:1]
    d_fields = spread * (
        d_hat
        - jnp.mean(d_hat, axis=-1, keepdims=True)
        - scaled * jnp.mean(d_hat * scaled, axis=-1, keepdims=True)
    )
    return d_next[rows, :] + d_fields, eight_rows(d_here * scaled)


def eight_rows(value):
    out = value[0:8]
    for at in range(8, value.shape[0], 8):
        out = out + value[at : at + 8]
    return out


def backward1_kernel(
    shifts_hbm,
    final_hbm,
    near_hbm,
    far_hbm,
    far_near_hbm,
    target_hbm,
    gain_hbm,
    noise_hbm,
    w_out_t_hbm,
    packed_hbm,
    weights_hbm,
    scaled_hbm,
    spread_hbm,
    w_qkv_t_hbm,
    east,
    west,
    d_out,
    head_out,
    gain_out,
    scale_out,
    shifts,
    final,
    near,
    far,
    far_near,
    target,
    gain,
    noise,
    w_out_t,
    packed,
    weights,
    scaled,
    spread,
    w_qkv_t,
    ext,
    d_next,
    d_mixed,
    d_packed,
    d_normed,
    sems,
):
    early = start_copies(
        sems,
        0,
        [
            (shifts_hbm, shifts),
            (target_hbm, target),
            (final_hbm, final),
            (near_hbm, near),
            (far_hbm, far),
            (far_near_hbm, far_near),
            (noise_hbm, noise),
        ],
    )
    copies = start_copies(
        sems,
        7,
        [(w_out_t_hbm, w_out_t), (packed_hbm, packed), (weights_hbm, weights)]
        + column_parts(w_qkv_t_hbm, w_qkv_t, 4),
    )
    late = start_copies(
        sems, 14, [(scaled_hbm, scaled), (spread_hbm, spread), (gain_hbm, gain)]
    )
    wait_all(early)
    fill(ext, target, west[...].astype(F32), east[...].astype(F32))
    for row in range(LAT):
        part = frame(ext, row, origin(shifts) + WIN, 16)
        for window in range(2):
            d_normed[window_rows(window, row), :] = part[window * WIN : (window + 1) * WIN]
    scale_total = jnp.zeros((8, C), F32)
    for at in range(0, ROWS, 32):
        rows = slice(at, at + 32)
        here = final[rows, :]
        pairs = (
            slope(here - near[rows, :].astype(F32))
            + slope(here - far[rows, :].astype(F32))
            + slope(here - far_near[rows, :].astype(F32))
        )
        seed = slope(here - d_normed[rows, :]) - pairs * (1.0 / 3.0)
        d_next[rows, :] = seed
        scale_total = scale_total + eight_rows(seed * noise[1, rows, :])
    step_back(copies, d_next, packed, weights, w_qkv_t, w_out_t, d_mixed, d_packed, d_normed)
    wait_all(late)
    gain_total = jnp.zeros((8, C), F32)
    for at in range(0, ROWS, 32):
        rows = slice(at, at + 32)
        d_here, gain_part = norm_back(at, d_next, scaled, spread, d_normed, gain[...])
        d_out[rows, :] = d_here
        if at < TOK:
            head_out[rows, :] = d_here.astype(BF16)
        gain_total = gain_total + gain_part
        scale_total = scale_total + eight_rows(d_here * noise[0, rows, :])
    gain_out[...] = gain_total
    scale_out[...] = scale_total


def backward0_kernel(
    shifts_hbm,
    gain_hbm,
    w_out_t_hbm,
    packed_hbm,
    weights_hbm,
    scaled_hbm,
    spread_hbm,
    w_qkv_t_hbm,
    d_in,
    d_east,
    gain_in,
    scale_in,
    own_out,
    tail_out,
    sums_out,
    shifts,
    gain,
    w_out_t,
    packed,
    weights,
    scaled,
    spread,
    w_qkv_t,
    ext,
    d_next,
    d_mixed,
    d_packed,
    d_normed,
    sems,
):
    early = start_copies(sems, 0, [(shifts_hbm, shifts)])
    copies = start_copies(
        sems,
        1,
        [(w_out_t_hbm, w_out_t), (packed_hbm, packed), (weights_hbm, weights)]
        + column_parts(w_qkv_t_hbm, w_qkv_t, 4),
    )
    late = start_copies(sems, 8, [(scaled_hbm, scaled), (spread_hbm, spread), (gain_hbm, gain)])
    wait_all(early)
    lon0, origin1 = shifts[0, 1], origin(shifts)
    east = d_east[...].astype(F32)
    for row in range(LAT):
        ext[row, 0:8, :] = d_in[row * WIN : (row + 1) * WIN, :]
        ext[row, 8:16, :] = d_in[TOK + row * WIN : TOK + (row + 1) * WIN, :]
        ext[row, 16:24, :] = east[row * WIN : (row + 1) * WIN]
    for row in range(LAT):
        part = frame(ext, row, lon0 - origin1, 16)
        for window in range(2):
            d_next[window_rows(window, row), :] = part[window * WIN : (window + 1) * WIN]
    step_back(copies, d_next, packed, weights, w_qkv_t, w_out_t, d_mixed, d_packed, d_normed)
    wait_all(late)
    gain_total = gain_in[...]
    for at in range(0, ROWS, 32):
        d_here, gain_part = norm_back(at, d_next, scaled, spread, d_normed, gain[...])
        gain_total = gain_total + gain_part
        for piece in range(4):
            token = at + piece * WIN
            row, window = (token % TOK) // WIN, token // TOK
            ext[row, 8 + window * WIN : 16 + window * WIN, :] = d_here[
                piece * WIN : (piece + 1) * WIN
            ]
    sums_out[0:1, :] = jnp.sum(gain_total, axis=0, keepdims=True)
    sums_out[1:2, :] = jnp.sum(scale_in[...], axis=0, keepdims=True)
    tails = []
    for row in range(LAT):
        own_out[row] = frame(ext, row, WIN - lon0, 16)
        tails.append(frame(ext, row, 24 - lon0, WIN))
    tail_out[...] = jnp.concatenate(tails, axis=0).astype(BF16)


WORK = [
    ((LAT, 32, C), F32),
    ((ROWS, C), F32),
    ((ROWS, C), BF16),
    ((ROWS, 3 * C), BF16),
    ((ROWS, C), F32),
]
SUMS = [((8, C), F32)] * 2


def backward1(shifts, final, others, target, east, west, noise, saved, gain, w_qkv_t, w_out_t):
    held = [
        ((ROWS, C), F32),
        ((ROWS, C), BF16),
        ((ROWS, C), BF16),
        ((ROWS, C), BF16),
        ((LAT, 16, C), F32),
        ((1, C), F32),
        ((2, ROWS, C), F32),
        ((C, C), BF16),
    ]
    return pl.pallas_call(
        backward1_kernel,
        out_shape=shapes([((ROWS, C), F32), ((TOK, C), BF16)] + SUMS),
        in_specs=[hbm()] * 14 + [vmem()] * 2,
        out_specs=[vmem()] * 4,
        scratch_shapes=[pltpu.SMEM((2, 2), jnp.int32)]
        + buffers(held + SAVED + [((3 * C, C), BF16)] + WORK)
        + [pltpu.SemaphoreType.DMA((17,))],
        compiler_params=compiler_params(),
        name="backward1",
    )(shifts, final, *others, target, gain, noise, w_out_t, *saved, w_qkv_t, east, west)


def backward0(shifts, d_in, d_east, saved, gain, gain_in, scale_in, w_qkv_t, w_out_t):
    return pl.pallas_call(
        backward0_kernel,
        out_shape=shapes([((LAT, 16, C), F32), ((TOK, C), BF16), ((2, C), F32)]),
        in_specs=[hbm()] * 8 + [vmem()] * 4,
        out_specs=[vmem()] * 3,
        scratch_shapes=[pltpu.SMEM((2, 2), jnp.int32), pltpu.VMEM((1, C), F32)]
        + buffers([((C, C), BF16)] + SAVED + [((3 * C, C), BF16)] + WORK)
        + [pltpu.SemaphoreType.DMA((11,))],
        compiler_params=compiler_params(),
        name="backward0",
    )(shifts, gain, w_out_t, *saved, w_qkv_t, d_in, d_east, gain_in, scale_in)


def along(value, axis, steps):
    count = lax.axis_size(axis)
    return lax.ppermute(value, axis, [(at, (at + steps) % count) for at in range(count)])


def swapped(value, axis, bit):
    count = lax.axis_size(axis)
    return lax.ppermute(value, axis, [(at, at ^ bit) for at in range(count)])


def total_over_devices(value, axis):
    bit = 1
    while bit < lax.axis_size(axis):
        value = value + swapped(value, axis, bit)
        bit *= 2
    return value


def local(initial, target, noise, w_qkv, w_out, gain, noise_scale, shifts):
    initial, noise = initial[0], noise[:, 0]

    def both_ways(part):
        shape = part.shape[:-3] + (TOK, C)
        first = part[..., :WIN, :].reshape(shape).astype(BF16)
        last = part[..., WIN:, :].reshape(shape).astype(BF16)
        return along(first, "tile", -1), along(last, "tile", 1)

    initial_sides = both_ways(initial)
    noise_sides = both_ways(noise)
    w_qkv_t, w_out_t = transposed(w_qkv), transposed(w_out)
    initial_sides, w_qkv_t, w_out_t = lax.optimization_barrier((initial_sides, w_qkv_t, w_out_t))
    gain_row, scale_row = gain[None], noise_scale[None]
    before, *saved0 = forward0(shifts, initial, *initial_sides, gain_row, w_qkv, w_out)
    noise_sides, target_now = lax.optimization_barrier((noise_sides, target))
    target_sides = both_ways(target_now)
    sent, final, noise_here, *saved1 = forward1(
        shifts, before, noise, *noise_sides, gain_row, scale_row, w_qkv, w_out
    )
    far = swapped(sent, "member", 2)
    near = swapped(sent, "member", 1)
    far_near = swapped(far, "member", 1)
    d_one, head, gain_part, scale_part = backward1(
        shifts,
        final,
        (near, far, far_near),
        target,
        *target_sides,
        noise_here,
        saved1,
        gain_row,
        w_qkv_t,
        w_out_t,
    )
    own, tail, sums = backward0(
        shifts,
        d_one,
        along(head, "tile", -1),
        saved0,
        gain_row,
        gain_part,
        scale_part,
        w_qkv_t,
        w_out_t,
    )
    arrived = along(tail, "tile", 1)
    sums = total_over_devices(sums, "member")
    sums, arrived = lax.optimization_barrier((sums, arrived))
    column = jnp.arange(WIN)[None, :, None]
    first = jnp.where(
        column < shifts[0, 1], arrived.reshape(LAT, WIN, C).astype(F32), own[:, :WIN]
    )
    state_grad = jnp.concatenate([first, own[:, WIN:]], axis=1)[None]
    sums = total_over_devices(sums, "tile")
    members = lax.axis_size("member")
    factor = (members * LAT * initial.shape[1] * lax.axis_size("tile")) ** (-0.5)
    return (state_grad, sums[0] * factor, sums[1] * factor)


def solution(mesh):
    in_specs = (
        P("member", None, "tile", None),
        P(None, "tile", None),
        P(None, "member", None, "tile", None),
        P(),
        P(),
        P(),
        P(),
        P(),
    )
    out_specs = (P("member", None, "tile", None), P(), P())
    return jax.shard_map(local, mesh=mesh, in_specs=in_specs, out_specs=out_specs, check_vma=False)
```

```python
import functools

import jax
import jax.numpy as jnp
from jax import lax
from jax.experimental import pallas as pl
from jax.experimental.pallas import tpu as pltpu
from jax.sharding import Mesh
from jax.sharding import PartitionSpec as P

C = 1024
HEAD = 32
WIN = 8
LAT = 8
TOK = LAT * WIN
GROUP = 4
LANES = GROUP * HEAD
GROUPS = C // LANES
SPAN = GROUP * TOK
SCALE = HEAD ** (-0.5)
SMOOTH = 0.25
F32 = jnp.float32
BF16 = jnp.bfloat16
VMEM_LIMIT = 14 * 1024 * 1024


def dot(left, right):
    return lax.dot_general(left, right, (((1,), (0,)), ((), ())), preferred_element_type=F32)


def dot_nt(left, right):
    return lax.dot_general(left, right, (((1,), (1,)), ((), ())), preferred_element_type=F32)


def dot_tn(left, right):
    return lax.dot_general(left, right, (((0,), (0,)), ((), ())), preferred_element_type=F32)


def head_masks():
    lane = lax.broadcasted_iota(jnp.int32, (TOK, LANES), 1) // HEAD
    return [lane == head for head in range(GROUP)]


def by_head(value, masks):
    zero = jnp.zeros_like(value)
    return jnp.concatenate([jnp.where(mask, value, zero) for mask in masks], axis=0)


def fold_heads(stacked, masks):
    out = stacked[:TOK]
    for head in range(1, GROUP):
        out = jnp.where(masks[head], stacked[head * TOK : (head + 1) * TOK], out)
    return out


def lat_mask(lat_shift):
    key_lat = lax.broadcasted_iota(jnp.int32, (TOK, SPAN), 0) // WIN
    query_lat = (lax.broadcasted_iota(jnp.int32, (TOK, SPAN), 1) % TOK) // WIN
    return (key_lat < lat_shift) == (query_lat < lat_shift)


def lanes(start, size):
    return pl.ds(pl.multiple_of(start, 128), size)


def fill(ext, own_ref, side, start):
    columns = side.shape[0] // LAT
    for row in range(LAT):
        ext[row, start : start + 16, :] = own_ref[row].astype(F32)
        ext[row, start + 16 : start + 16 + columns, :] = side[
            row * columns : (row + 1) * columns
        ]


def side_rows(ref, part):
    return ref[part * TOK : (part + 1) * TOK, :].astype(F32)


def frame(ext, row, start, columns):
    held = ext.shape[1]
    return pltpu.roll(ext[row], lax.rem(held - start, held), 0)[:columns]


def norm_rows(x_ref, rows, gain, normed_ref, scaled_ref, spread_ref, saved_from):
    for at in range(0, rows, 32):
        x = x_ref[at : at + 32, :]
        centre = jnp.mean(x, axis=-1, keepdims=True)
        offset = x - centre
        spread = lax.rsqrt(jnp.mean(offset * offset, axis=-1, keepdims=True) + 1e-05)
        scaled = offset * spread
        normed_ref[at : at + 32, :] = (scaled * gain).astype(BF16)
        if at >= saved_from:
            scaled_ref[at - saved_from : at - saved_from + 32, :] = scaled.astype(BF16)
            spread_ref[at - saved_from : at - saved_from + 32, :] = jnp.broadcast_to(
                spread, (32, 128)
            )


def attend(windows, packed_ref, weights_ref, mixed_ref, lat_shift, saved_from):
    masks = head_masks()
    allowed = lat_mask(lat_shift)

    def group(at, _):
        for window in range(windows):
            rows = slice(window * TOK, (window + 1) * TOK)
            queries = packed_ref[rows, lanes(at * LANES, LANES)]
            keys = packed_ref[rows, lanes(C + at * LANES, LANES)]
            values = packed_ref[rows, lanes(2 * C + at * LANES, LANES)]
            scores = dot_nt(keys, by_head(queries, masks))
            scores = jnp.where(allowed, scores, -1e9 / SCALE)
            highest = jnp.max(scores, axis=0, keepdims=True)
            raised = jnp.exp((scores - highest) * SCALE)
            total = jnp.sum(raised, axis=0, keepdims=True)
            weights = (raised * (1.0 / total)).astype(BF16)
            if window >= saved_from:
                weights_ref[(window - saved_from) * GROUPS + at] = weights
            mixed = fold_heads(dot_tn(weights, values), masks)
            mixed_ref[rows, lanes(at * LANES, LANES)] = mixed.astype(BF16)
        return 0

    lax.fori_loop(0, GROUPS, group, 0, unroll=GROUPS)


def window_rows(window, row):
    start = window * TOK + row * WIN
    return slice(start, start + WIN)


def start_copies(sems, first, pairs):
    copies = []
    for at, (source, destination) in enumerate(pairs):
        copy = pltpu.make_async_copy(source, destination, sems.at[first + at])
        copy.start()
        copies.append(copy)
    return copies


def wait_all(copies):
    for copy in copies:
        copy.wait()


def column_parts(source, destination, parts):
    width = source.shape[1] // parts
    return [
        (source.at[:, pl.ds(at * width, width)], destination.at[:, pl.ds(at * width, width)])
        for at in range(parts)
    ]


def forward0_kernel(
    initial_hbm,
    shifts_hbm,
    gain_hbm,
    w_qkv,
    w_out,
    east,
    west,
    following_out,
    packed_hbm,
    weights_hbm,
    scaled_hbm,
    spread_hbm,
    initial,
    shifts,
    gain,
    ext,
    state,
    normed,
    packed,
    mixed,
    weights,
    scaled,
    spread,
    sems,
):
    small = start_copies(
        sems, 0, [(shifts_hbm, shifts), (initial_hbm, initial), (gain_hbm, gain)]
    )
    wait_all(small)
    lat_shift = shifts[0, 0]
    fill(ext, initial, east[0 : 2 * TOK, :].astype(F32), WIN)
    before = west[...].astype(F32)
    for row in range(LAT):
        ext[row, 0:WIN, :] = before[row * WIN : (row + 1) * WIN]
        part = frame(ext, row, origin0(shifts) + WIN, 24)
        for window in range(3):
            state[window_rows(window, row), :] = part[window * WIN : (window + 1) * WIN]
    norm_rows(state, 3 * TOK, gain[...], normed, scaled, spread, TOK)
    saves = start_copies(sems, 3, [(scaled, scaled_hbm), (spread, spread_hbm)])
    for part in range(6):
        at = slice(part * 512, (part + 1) * 512)
        packed[:, at] = dot(normed[...], w_qkv[:, at]).astype(BF16)
    saves += start_copies(sems, 5, [(packed.at[pl.ds(TOK, 2 * TOK)], packed_hbm)])
    attend(3, packed, weights, mixed, lat_shift, 1)
    saves += start_copies(sems, 6, [(weights, weights_hbm)])
    for part in range(4):
        at = slice(part * 256, (part + 1) * 256)
        following = state[:, at] + dot(mixed[...], w_out[:, at])
        for row in range(LAT):
            for window in range(3):
                following_out[row, window * WIN : (window + 1) * WIN, at] = following[
                    window_rows(window, row)
                ]
    wait_all(saves)


def forward1_kernel(
    noise_hbm,
    shifts_hbm,
    gain_hbm,
    scale_hbm,
    w_qkv,
    w_out,
    before,
    east,
    sent_out,
    final_hbm,
    noise_out_hbm,
    packed_hbm,
    weights_hbm,
    scaled_hbm,
    spread_hbm,
    noise,
    shifts,
    gain,
    noise_scale,
    ext,
    state,
    final,
    noise_here,
    normed,
    packed,
    mixed,
    weights,
    scaled,
    spread,
    sems,
):
    small = start_copies(
        sems,
        0,
        [(shifts_hbm, shifts), (noise_hbm, noise), (gain_hbm, gain), (scale_hbm, noise_scale)],
    )
    wait_all(small)
    lat_shift = shifts[1, 0]
    lon1 = shifts[1, 1]
    scale = noise_scale[...]
    for step in range(2):
        fill(ext, noise.at[step], side_rows(east, 2 + step), 0)
        for row in range(LAT):
            part = frame(ext, row, lon1, 16)
            if step == 0:
                fields = frame(before, row, lon1 - origin0(shifts), 16)
            for window in range(2):
                rows = window_rows(window, row)
                here = part[window * WIN : (window + 1) * WIN]
                if step == 0:
                    state[rows, :] = fields[window * WIN : (window + 1) * WIN] + scale * here
                else:
                    final[rows, :] = state[rows, :] + scale * here
                noise_here[step, rows, :] = here
    saves = start_copies(sems, 4, [(noise_here, noise_out_hbm)])
    norm_rows(state, 2 * TOK, gain[...], normed, scaled, spread, 0)
    saves += start_copies(sems, 5, [(scaled, scaled_hbm), (spread, spread_hbm)])
    for part in range(6):
        at = slice(part * 512, (part + 1) * 512)
        packed[:, at] = dot(normed[...], w_qkv[:, at]).astype(BF16)
    saves += start_copies(sems, 7, [(packed, packed_hbm)])
    attend(2, packed, weights, mixed, lat_shift, 0)
    saves += start_copies(sems, 8, [(weights, weights_hbm)])
    for part in range(4):
        at = slice(part * 256, (part + 1) * 256)
        last = final[:, at] + dot(mixed[...], w_out[:, at])
        final[:, at] = last
        sent_out[:, at] = last.astype(BF16)
    saves += start_copies(sems, 9, [(final, final_hbm)])
    wait_all(saves)


def origin0(shifts):
    lon0, lon1 = shifts[0, 1], shifts[1, 1]
    return jnp.where(lon0 <= lon1, lon0, lon0 - WIN)


def vmem():
    return pl.BlockSpec(memory_space=pltpu.VMEM)


def hbm():
    return pl.BlockSpec(memory_space=pltpu.HBM)


def compiler_params():
    return pltpu.CompilerParams(vmem_limit_bytes=VMEM_LIMIT)


ROWS = 2 * TOK
SAVED = [
    ((ROWS, 3 * C), BF16),
    ((2 * GROUPS, TOK, SPAN), BF16),
    ((ROWS, C), BF16),
    ((ROWS, 128), F32),
]


def shapes(entries):
    return [jax.ShapeDtypeStruct(shape, dtype) for shape, dtype in entries]


def buffers(entries):
    return [pltpu.VMEM(shape, dtype) for shape, dtype in entries]


WEIGHTS = [((C, 3 * C), BF16), ((C, C), BF16)]


def forward0(shifts, initial, east, west, gain, w_qkv, w_out):
    rows = 3 * TOK
    return pl.pallas_call(
        forward0_kernel,
        out_shape=shapes([((LAT, 24, C), F32)] + SAVED),
        in_specs=[hbm()] * 3 + [vmem()] * 4,
        out_specs=[vmem()] + [hbm()] * 4,
        scratch_shapes=[
            pltpu.VMEM((LAT, 16, C), F32),
            pltpu.SMEM((2, 2), jnp.int32),
            pltpu.VMEM((1, C), F32),
        ]
        + buffers(
            [
                ((LAT, 40, C), F32),
                ((rows, C), F32),
                ((rows, C), BF16),
                ((rows, 3 * C), BF16),
                ((rows, C), BF16),
            ]
        )
        + buffers(SAVED[1:])
        + [pltpu.SemaphoreType.DMA((7,))],
        compiler_params=compiler_params(),
        name="forward0",
    )(initial, shifts, gain, w_qkv, w_out, east, west)


def forward1(shifts, before, noise, east, gain, noise_scale, w_qkv, w_out):
    return pl.pallas_call(
        forward1_kernel,
        out_shape=shapes([((ROWS, C), BF16), ((ROWS, C), F32), ((2, ROWS, C), F32)] + SAVED),
        in_specs=[hbm()] * 4 + [vmem()] * 4,
        out_specs=[vmem()] + [hbm()] * 6,
        scratch_shapes=[
            pltpu.VMEM((2, LAT, 16, C), BF16),
            pltpu.SMEM((2, 2), jnp.int32),
            pltpu.VMEM((1, C), F32),
            pltpu.VMEM((1, C), F32),
        ]
        + buffers(
            [
                ((LAT, 24, C), F32),
                ((ROWS, C), F32),
                ((ROWS, C), F32),
                ((2, ROWS, C), F32),
                ((ROWS, C), BF16),
                ((ROWS, 3 * C), BF16),
                ((ROWS, C), BF16),
            ]
        )
        + buffers(SAVED[1:])
        + [pltpu.SemaphoreType.DMA((10,))],
        compiler_params=compiler_params(),
        name="forward1",
    )(noise, shifts, gain, noise_scale, w_qkv, w_out, before, east)


def prepare_kernel(w_qkv_hbm, w_out_hbm, w_qkv, w_out, w_qkv_t, w_out_t, sems):
    copies = start_copies(sems, 0, column_parts(w_qkv_hbm, w_qkv, 6))
    copies += start_copies(sems, 6, column_parts(w_out_hbm, w_out, 2))
    for part in range(8):
        copies[part].wait()
        held, turned = (w_qkv, w_qkv_t) if part < 6 else (w_out, w_out_t)
        at = part % 6 * 512
        turned[at : at + 512, :] = held[:, at : at + 512].T


def prepare(w_qkv, w_out):
    return pl.pallas_call(
        prepare_kernel,
        out_shape=shapes(WEIGHTS + [((3 * C, C), BF16), ((C, C), BF16)]),
        in_specs=[hbm()] * 2,
        out_specs=[vmem()] * 4,
        scratch_shapes=[pltpu.SemaphoreType.DMA((8,))],
        compiler_params=compiler_params(),
        name="prepare",
    )(w_qkv, w_out)


def borders_kernel(initial_hbm, noise_hbm, target_hbm, east, west, initial, noise, target, sems):
    copies = start_copies(
        sems, 0, [(initial_hbm, initial), (noise_hbm, noise), (target_hbm, target)]
    )

    def rows(held, first, columns):
        parts = [held[row].astype(F32)[first : first + columns] for row in range(LAT)]
        return jnp.concatenate(parts).astype(BF16)

    copies[0].wait()
    east[0 : 2 * TOK, :] = rows(initial, 0, 16)
    west[...] = rows(initial, WIN, WIN)
    copies[1].wait()
    east[2 * TOK : 3 * TOK, :] = rows(noise.at[0], 0, WIN)
    east[3 * TOK : 4 * TOK, :] = rows(noise.at[1], 0, WIN)
    copies[2].wait()
    east[4 * TOK : 5 * TOK, :] = rows(target, 0, WIN)


def borders(initial, noise, target):
    return pl.pallas_call(
        borders_kernel,
        out_shape=shapes([((5 * TOK, C), BF16), ((TOK, C), BF16)]),
        in_specs=[hbm()] * 3,
        out_specs=[vmem()] * 2,
        scratch_shapes=buffers(
            [((LAT, 16, C), F32), ((2, LAT, 16, C), BF16), ((LAT, 16, C), F32)]
        )
        + [pltpu.SemaphoreType.DMA((3,))],
        compiler_params=pltpu.CompilerParams(vmem_limit_bytes=56 * 1024 * 1024),
        name="borders",
    )(initial, noise, target)


def attend_back(packed, weights_ref, d_mixed, d_packed):
    masks = head_masks()

    def group(at, _):
        for window in range(2):
            rows = slice(window * TOK, (window + 1) * TOK)
            here = lanes(at * LANES, LANES)
            queries = packed[rows, here]
            keys = packed[rows, lanes(C + at * LANES, LANES)]
            values = packed[rows, lanes(2 * C + at * LANES, LANES)]
            d_mixed_blocks = by_head(d_mixed[rows, here], masks)
            weights = weights_ref[window * GROUPS + at]
            d_weights = dot_nt(values, d_mixed_blocks)
            d_values = dot(weights, d_mixed_blocks)
            probs = weights.astype(F32)
            centred = d_weights - jnp.sum(d_weights * probs, axis=0, keepdims=True)
            d_scores = (probs * centred * SCALE).astype(BF16)
            d_keys = dot(d_scores, by_head(queries, masks))
            d_queries = fold_heads(dot_tn(d_scores, keys), masks)
            d_packed[rows, here] = d_queries.astype(BF16)
            d_packed[rows, lanes(C + at * LANES, LANES)] = d_keys.astype(BF16)
            d_packed[rows, lanes(2 * C + at * LANES, LANES)] = d_values.astype(BF16)
        return 0

    lax.fori_loop(0, GROUPS, group, 0, unroll=GROUPS)


def slope(difference):
    return difference * lax.rsqrt(difference * difference + SMOOTH * SMOOTH)


def step_back(
    copies, d_next, packed, weights, w_qkv_t, w_out_t, d_mixed, d_packed, d_normed
):
    d_branch = d_next[...].astype(BF16)
    for part in range(4):
        at = slice(part * 256, (part + 1) * 256)
        d_mixed[:, at] = dot(d_branch, w_out_t[:, at]).astype(BF16)
    wait_all(copies)
    attend_back(packed, weights, d_mixed, d_packed)
    for part in range(4):
        at = slice(part * 256, (part + 1) * 256)
        d_normed[:, at] = dot(d_packed[...], w_qkv_t[:, at])


def norm_back(at, d_next, scaled_ref, spread_ref, d_normed, gain):
    rows = slice(at, at + 32)
    scaled = scaled_ref[rows, :].astype(F32)
    d_here = d_normed[rows, :]
    d_hat = d_here * gain
    spread = spread_ref[rows, 0:1]
    d_fields = spread * (
        d_hat
        - jnp.mean(d_hat, axis=-1, keepdims=True)
        - scaled * jnp.mean(d_hat * scaled, axis=-1, keepdims=True)
    )
    return d_next[rows, :] + d_fields, eight_rows(d_here * scaled)


def eight_rows(value):
    out = value[0:8]
    for at in range(8, value.shape[0], 8):
        out = out + value[at : at + 8]
    return out


def backward1_kernel(
    shifts_hbm,
    final_hbm,
    near_hbm,
    far_hbm,
    far_near_hbm,
    target_hbm,
    gain_hbm,
    noise_hbm,
    packed_hbm,
    weights_hbm,
    scaled_hbm,
    spread_hbm,
    w_out_t,
    w_qkv_t,
    east,
    d_out,
    head_out,
    gain_out,
    scale_out,
    shifts,
    final,
    near,
    far,
    far_near,
    target,
    gain,
    noise,
    packed,
    weights,
    scaled,
    spread,
    ext,
    d_next,
    d_mixed,
    d_packed,
    d_normed,
    sems,
):
    early = start_copies(
        sems,
        0,
        [
            (shifts_hbm, shifts),
            (target_hbm, target),
            (final_hbm, final),
            (near_hbm, near),
            (far_hbm, far),
            (far_near_hbm, far_near),
            (noise_hbm, noise),
        ],
    )
    copies = start_copies(
        sems,
        7,
        [(packed_hbm, packed), (weights_hbm, weights)],
    )
    late = start_copies(
        sems, 9, [(scaled_hbm, scaled), (spread_hbm, spread), (gain_hbm, gain)]
    )
    wait_all(early)
    fill(ext, target, side_rows(east, 4), 0)
    for row in range(LAT):
        part = frame(ext, row, shifts[1, 1], 16)
        for window in range(2):
            d_normed[window_rows(window, row), :] = part[window * WIN : (window + 1) * WIN]
    scale_total = jnp.zeros((8, C), F32)
    for at in range(0, ROWS, 32):
        rows = slice(at, at + 32)
        here = final[rows, :]
        pairs = (
            slope(here - near[rows, :].astype(F32))
            + slope(here - far[rows, :].astype(F32))
            + slope(here - far_near[rows, :].astype(F32))
        )
        seed = slope(here - d_normed[rows, :]) - pairs * (1.0 / 3.0)
        d_next[rows, :] = seed
        scale_total = scale_total + eight_rows(seed * noise[1, rows, :])
    step_back(copies, d_next, packed, weights, w_qkv_t, w_out_t, d_mixed, d_packed, d_normed)
    wait_all(late)
    gain_total = jnp.zeros((8, C), F32)
    for at in range(0, ROWS, 32):
        rows = slice(at, at + 32)
        d_here, gain_part = norm_back(at, d_next, scaled, spread, d_normed, gain[...])
        d_out[rows, :] = d_here
        if at < TOK:
            head_out[rows, :] = d_here.astype(BF16)
        gain_total = gain_total + gain_part
        scale_total = scale_total + eight_rows(d_here * noise[0, rows, :])
    gain_out[...] = gain_total
    scale_out[...] = scale_total


def backward0_kernel(
    shifts_hbm,
    gain_hbm,
    packed_hbm,
    weights_hbm,
    scaled_hbm,
    spread_hbm,
    w_out_t,
    w_qkv_t,
    d_in,
    d_east,
    gain_in,
    scale_in,
    own_out,
    tail_out,
    sums_out,
    shifts,
    gain,
    packed,
    weights,
    scaled,
    spread,
    ext,
    d_next,
    d_mixed,
    d_packed,
    d_normed,
    sems,
):
    early = start_copies(sems, 0, [(shifts_hbm, shifts)])
    copies = start_copies(
        sems,
        1,
        [(packed_hbm, packed), (weights_hbm, weights)],
    )
    late = start_copies(sems, 3, [(scaled_hbm, scaled), (spread_hbm, spread), (gain_hbm, gain)])
    wait_all(early)
    start = origin0(shifts) + WIN
    east = d_east[...].astype(F32)
    for row in range(LAT):
        ext[row, 0:8, :] = d_in[row * WIN : (row + 1) * WIN, :]
        ext[row, 8:16, :] = d_in[TOK + row * WIN : TOK + (row + 1) * WIN, :]
        ext[row, 16:24, :] = east[row * WIN : (row + 1) * WIN]
    for row in range(LAT):
        part = frame(ext, row, start - shifts[1, 1], 16)
        for window in range(2):
            d_next[window_rows(window, row), :] = part[window * WIN : (window + 1) * WIN]
    step_back(copies, d_next, packed, weights, w_qkv_t, w_out_t, d_mixed, d_packed, d_normed)
    wait_all(late)
    gain_total = gain_in[...]
    for at in range(0, ROWS, 32):
        d_here, gain_part = norm_back(at, d_next, scaled, spread, d_normed, gain[...])
        gain_total = gain_total + gain_part
        for piece in range(4):
            token = at + piece * WIN
            row, window = (token % TOK) // WIN, token // TOK
            ext[row, 16 + window * WIN : 24 + window * WIN, :] = d_here[
                piece * WIN : (piece + 1) * WIN
            ]
    sums_out[0:1, :] = jnp.sum(gain_total, axis=0, keepdims=True)
    sums_out[1:2, :] = jnp.sum(scale_in[...], axis=0, keepdims=True)
    tails = []
    for row in range(LAT):
        own_out[row] = frame(ext, row, 16 - start, 16)
        tails.append(frame(ext, row, 32 - start, 16))
    tail_out[...] = jnp.concatenate(tails, axis=0).astype(BF16)


WORK = [
    ((LAT, 24, C), F32),
    ((ROWS, C), F32),
    ((ROWS, C), BF16),
    ((ROWS, 3 * C), BF16),
    ((ROWS, C), F32),
]
SUMS = [((8, C), F32)] * 2


def backward1(shifts, final, others, target, east, noise, saved, gain, w_qkv_t, w_out_t):
    held = [
        ((ROWS, C), F32),
        ((ROWS, C), BF16),
        ((ROWS, C), BF16),
        ((ROWS, C), BF16),
        ((LAT, 16, C), F32),
        ((1, C), F32),
        ((2, ROWS, C), F32),
    ]
    return pl.pallas_call(
        backward1_kernel,
        out_shape=shapes([((ROWS, C), F32), ((TOK, C), BF16)] + SUMS),
        in_specs=[hbm()] * 12 + [vmem()] * 3,
        out_specs=[vmem()] * 4,
        scratch_shapes=[pltpu.SMEM((2, 2), jnp.int32)]
        + buffers(held + SAVED + WORK)
        + [pltpu.SemaphoreType.DMA((12,))],
        compiler_params=compiler_params(),
        name="backward1",
    )(shifts, final, *others, target, gain, noise, *saved, w_out_t, w_qkv_t, east)


def backward0(shifts, d_in, d_east, saved, gain, gain_in, scale_in, w_qkv_t, w_out_t):
    return pl.pallas_call(
        backward0_kernel,
        out_shape=shapes([((LAT, 16, C), F32), ((ROWS, C), BF16), ((2, C), F32)]),
        in_specs=[hbm()] * 6 + [vmem()] * 6,
        out_specs=[vmem()] * 3,
        scratch_shapes=[pltpu.SMEM((2, 2), jnp.int32), pltpu.VMEM((1, C), F32)]
        + buffers(SAVED + [((LAT, 48, C), F32)] + WORK[1:])
        + [pltpu.SemaphoreType.DMA((6,))],
        compiler_params=compiler_params(),
        name="backward0",
    )(shifts, gain, *saved, w_out_t, w_qkv_t, d_in, d_east, gain_in, scale_in)


MEMBER = ("pair", "core")
TILE = ("far", "row", "half")


def along(value, steps):
    count = lax.axis_size(TILE)
    return lax.ppermute(value, TILE, [(at, (at + steps) % count) for at in range(count)])


def other(value, axis):
    return lax.ppermute(value, axis, [(0, 1), (1, 0)])


def total_over(value, axes):
    count = lax.axis_size(axes)
    copies = jnp.broadcast_to(value[None], (count,) + value.shape)
    return jnp.sum(lax.all_to_all(copies, axes, 0, 0), axis=0)


def local(initial, target, noise, w_qkv, w_out, gain, noise_scale, shifts):
    initial, noise = initial[0], noise[:, 0]
    gain_row, scale_row = gain[None], noise_scale[None]
    east, west = borders(initial, noise, target)
    east, west = along(east, -1), along(west, 1)
    prepared = prepare(w_qkv, w_out)
    east, west, prepared = lax.optimization_barrier((east, west, prepared))
    here, here_t = prepared[:2], prepared[2:]
    before, *saved0 = forward0(shifts, initial, east, west, gain_row, *here)
    sent, final, noise_here, *saved1 = forward1(
        shifts, before, noise, east, gain_row, scale_row, *here
    )
    far = other(sent, "pair")
    near = other(sent, "core")
    far_near = other(far, "core")
    d_one, head, gain_part, scale_part = backward1(
        shifts,
        final,
        (near, far, far_near),
        target,
        east,
        noise_here,
        saved1,
        gain_row,
        *here_t,
    )
    own, tail, sums = backward0(
        shifts, d_one, along(head, -1), saved0, gain_row, gain_part, scale_part, *here_t
    )
    arrived = along(tail, 1)
    sums = total_over(sums, MEMBER + TILE[1:])
    sums, arrived = lax.optimization_barrier((sums, arrived))
    sums = total_over(sums, TILE[0])
    column = jnp.arange(16)[None, :, None]
    state_grad = jnp.where(
        column < origin0(shifts) + WIN, arrived.reshape(LAT, 16, C).astype(F32), own
    )[None]
    members = lax.axis_size(MEMBER)
    factor = (members * LAT * initial.shape[1] * lax.axis_size(TILE)) ** (-0.5)
    return (state_grad, sums[0] * factor, sums[1] * factor)


def solution(mesh):
    members, tiles = mesh.devices.shape
    fine = Mesh(mesh.devices.reshape(members // 2, 2, tiles // 8, 4, 2), MEMBER + TILE)
    in_specs = (
        P(MEMBER, None, TILE, None),
        P(None, TILE, None),
        P(None, MEMBER, None, TILE, None),
        P(),
        P(),
        P(),
        P(),
        P(),
    )
    out_specs = (P(MEMBER, None, TILE, None), P(), P())
    return jax.shard_map(local, mesh=fine, in_specs=in_specs, out_specs=out_specs, check_vma=False)
```

```python
import functools

import jax
import jax.numpy as jnp
from jax import lax
from jax.experimental import pallas as pl
from jax.experimental.pallas import tpu as pltpu
from jax.sharding import Mesh
from jax.sharding import PartitionSpec as P

C = 1024
HEAD = 32
WIN = 8
LAT = 8
TOK = LAT * WIN
GROUP = 4
LANES = GROUP * HEAD
GROUPS = C // LANES
SPAN = GROUP * TOK
SCALE = HEAD ** (-0.5)
SMOOTH = 0.25
F32 = jnp.float32
BF16 = jnp.bfloat16
VMEM_LIMIT = 14 * 1024 * 1024


def dot(left, right):
    return lax.dot_general(left, right, (((1,), (0,)), ((), ())), preferred_element_type=F32)


def dot_nt(left, right):
    return lax.dot_general(left, right, (((1,), (1,)), ((), ())), preferred_element_type=F32)


def dot_tn(left, right):
    return lax.dot_general(left, right, (((0,), (0,)), ((), ())), preferred_element_type=F32)


def head_masks():
    lane = lax.broadcasted_iota(jnp.int32, (TOK, LANES), 1) // HEAD
    return [lane == head for head in range(GROUP)]


def by_head(value, masks):
    zero = jnp.zeros_like(value)
    return jnp.concatenate([jnp.where(mask, value, zero) for mask in masks], axis=0)


def fold_heads(stacked, masks):
    out = stacked[:TOK]
    for head in range(1, GROUP):
        out = jnp.where(masks[head], stacked[head * TOK : (head + 1) * TOK], out)
    return out


def lat_mask(lat_shift):
    key_lat = lax.broadcasted_iota(jnp.int32, (TOK, SPAN), 0) // WIN
    query_lat = (lax.broadcasted_iota(jnp.int32, (TOK, SPAN), 1) % TOK) // WIN
    return (key_lat < lat_shift) == (query_lat < lat_shift)


def lanes(start, size):
    return pl.ds(pl.multiple_of(start, 128), size)


def fill(ext, own_ref, side, start):
    columns = side.shape[0] // LAT
    for row in range(LAT):
        ext[row, start : start + 16, :] = own_ref[row].astype(F32)
        ext[row, start + 16 : start + 16 + columns, :] = side[
            row * columns : (row + 1) * columns
        ]


NOISE_ROWS = LAT * 7
PART_ROWS = TOK // 4
EAST_INITIAL = 2 * NOISE_ROWS + PART_ROWS
INITIAL_ROWS = LAT * 15
EAST_ROWS = 256
SENT_ROWS = 2 * TOK + PART_ROWS
QUARTER = C // 4


def member_index():
    return lax.axis_index("pair") * 2 + lax.axis_index("core")


def quarter(member):
    return pl.ds(pl.multiple_of(member * QUARTER, QUARTER), QUARTER)


def frame(ext, row, start, columns):
    held = ext.shape[1]
    return pltpu.roll(ext[row], lax.rem(held - start, held), 0)[:columns]


def norm_rows(x_ref, rows, gain, normed_ref, scaled_ref, spread_ref, saved):
    for at in range(0, rows, 32):
        x = x_ref[at : at + 32, :]
        centre = jnp.mean(x, axis=-1, keepdims=True)
        offset = x - centre
        spread = lax.rsqrt(jnp.mean(offset * offset, axis=-1, keepdims=True) + 1e-05)
        scaled = offset * spread
        normed_ref[at : at + 32, :] = (scaled * gain).astype(BF16)
        if at < saved:
            scaled_ref[at : at + 32, :] = scaled.astype(BF16)
            spread_ref[at : at + 32, :] = jnp.broadcast_to(spread, (32, 128))


def attend(windows, packed_ref, weights_ref, mixed_ref, lat_shift, saved):
    masks = head_masks()
    allowed = lat_mask(lat_shift)

    def group(at, _):
        for window in range(windows):
            rows = slice(window * TOK, (window + 1) * TOK)
            queries = packed_ref[rows, lanes(at * LANES, LANES)]
            keys = packed_ref[rows, lanes(C + at * LANES, LANES)]
            values = packed_ref[rows, lanes(2 * C + at * LANES, LANES)]
            scores = dot_nt(keys, by_head(queries, masks))
            scores = jnp.where(allowed, scores, -1e9 / SCALE)
            highest = jnp.max(scores, axis=0, keepdims=True)
            raised = jnp.exp((scores - highest) * SCALE)
            total = jnp.sum(raised, axis=0, keepdims=True)
            weights = (raised * (1.0 / total)).astype(BF16)
            if window < saved:
                weights_ref[window * GROUPS + at] = weights
            mixed = fold_heads(dot_tn(weights, values), masks)
            mixed_ref[rows, lanes(at * LANES, LANES)] = mixed.astype(BF16)
        return 0

    lax.fori_loop(0, GROUPS, group, 0, unroll=GROUPS)


def window_rows(window, row):
    start = window * TOK + row * WIN
    return slice(start, start + WIN)


def start_copies(sems, first, pairs):
    copies = []
    for at, (source, destination) in enumerate(pairs):
        copy = pltpu.make_async_copy(source, destination, sems.at[first + at])
        copy.start()
        copies.append(copy)
    return copies


def wait_all(copies):
    for copy in copies:
        copy.wait()


def column_parts(source, destination, parts):
    width = source.shape[1] // parts
    return [
        (source.at[:, pl.ds(at * width, width)], destination.at[:, pl.ds(at * width, width)])
        for at in range(parts)
    ]


def forward0_kernel(
    shifts_hbm,
    initial,
    gain,
    w_qkv,
    w_out,
    east,
    west,
    following_out,
    packed_out,
    weights_out,
    scaled_out,
    spread_out,
    shifts,
    ext,
    state,
    normed,
    packed,
    mixed,
    sems,
):
    small = start_copies(sems, 0, [(shifts_hbm, shifts)])
    fill(ext, initial, east[EAST_INITIAL:, :].astype(F32)[:INITIAL_ROWS], WIN)
    before = west[...].astype(F32)
    for row in range(LAT):
        ext[row, 0:WIN, :] = before[row * WIN : (row + 1) * WIN]
    wait_all(small)
    lat_shift = shifts[0, 0]
    for row in range(LAT):
        part = frame(ext, row, shifts[0, 1], 32)
        for window in range(4):
            state[window_rows(window, row), :] = part[window * WIN : (window + 1) * WIN]
    norm_rows(state, 4 * TOK, gain[...], normed, scaled_out, spread_out, 3 * TOK)
    for part in range(6):
        at = slice(part * 512, (part + 1) * 512)
        packed[:, at] = dot(normed[...], w_qkv[:, at]).astype(BF16)
    packed_out[...] = packed[: 3 * TOK, :]
    attend(4, packed, weights_out, mixed, lat_shift, 3)
    for part in range(4):
        at = slice(part * 256, (part + 1) * 256)
        following = state[:, at] + dot(mixed[...], w_out[:, at])
        for row in range(LAT):
            for window in range(4):
                following_out[row, window * WIN : (window + 1) * WIN, at] = following[
                    window_rows(window, row)
                ]


def forward1_kernel(
    shifts_hbm,
    noise,
    gain,
    noise_scale,
    w_qkv,
    w_out,
    before,
    east,
    sent_out,
    final,
    noise_here,
    packed,
    weights,
    scaled,
    spread,
    shifts,
    ext,
    state,
    normed,
    mixed,
    sems,
):
    small = start_copies(sems, 0, [(shifts_hbm, shifts)])
    side = east[: 2 * NOISE_ROWS, :].astype(F32)
    fill(ext, noise.at[0], side[:NOISE_ROWS], 0)
    wait_all(small)
    lat_shift, lon1 = shifts[1, 0], shifts[1, 1]
    scale = noise_scale[...]
    for row in range(LAT):
        part = frame(ext, row, lon1, 16)
        fields = frame(before, row, lon1 - shifts[0, 1] + WIN, 16)
        for window in range(2):
            rows = window_rows(window, row)
            here = part[window * WIN : (window + 1) * WIN]
            state[rows, :] = fields[window * WIN : (window + 1) * WIN] + scale * here
            noise_here[0, rows, :] = here
    fill(ext, noise.at[1], side[NOISE_ROWS:], 0)
    for row in range(LAT):
        part = frame(ext, row, lon1, 16)
        for window in range(2):
            rows = window_rows(window, row)
            here = part[window * WIN : (window + 1) * WIN]
            final[rows, :] = state[rows, :] + scale * here
            noise_here[1, rows, :] = here
    norm_rows(state, 2 * TOK, gain[...], normed, scaled, spread, 2 * TOK)
    for part in range(6):
        at = slice(part * 512, (part + 1) * 512)
        packed[:, at] = dot(normed[...], w_qkv[:, at]).astype(BF16)
    attend(2, packed, weights, mixed, lat_shift, 2)
    for part in range(4):
        at = slice(part * 256, (part + 1) * 256)
        last = final[:, at] + dot(mixed[...], w_out[:, at])
        final[:, at] = last
        sent_out[0:ROWS, at] = last.astype(BF16)
    sent_out[ROWS:SENT_ROWS, :] = east[2 * NOISE_ROWS : EAST_INITIAL, :]


def vmem():
    return pl.BlockSpec(memory_space=pltpu.VMEM)


def hbm():
    return pl.BlockSpec(memory_space=pltpu.HBM)


def cost(microseconds):
    return pl.CostEstimate(
        flops=0, bytes_accessed=int(microseconds * 3_500_000), transcendentals=0
    )


def compiler_params():
    return pltpu.CompilerParams(vmem_limit_bytes=VMEM_LIMIT)


ROWS = 2 * TOK


def saved(windows):
    return [
        ((windows * TOK, 3 * C), BF16),
        ((windows * GROUPS, TOK, SPAN), BF16),
        ((windows * TOK, C), BF16),
        ((windows * TOK, 128), F32),
    ]


def shapes(entries):
    return [jax.ShapeDtypeStruct(shape, dtype) for shape, dtype in entries]


def buffers(entries):
    return [pltpu.VMEM(shape, dtype) for shape, dtype in entries]


WEIGHTS = [((C, 3 * C), BF16), ((C, C), BF16)]


def shifts_buffers():
    return [pltpu.SMEM((2, 2), jnp.int32)]


def forward0(shifts, initial, east, west, gain, w_qkv, w_out):
    rows = 4 * TOK
    return pl.pallas_call(
        forward0_kernel,
        out_shape=shapes([((LAT, 32, C), F32)] + saved(3)),
        in_specs=[hbm()] + [vmem()] * 6,
        out_specs=[vmem()] * 5,
        scratch_shapes=shifts_buffers()
        + buffers(
            [
                ((LAT, 40, C), F32),
                ((rows, C), F32),
                ((rows, C), BF16),
                ((rows, 3 * C), BF16),
                ((rows, C), BF16),
            ]
        )
        + [pltpu.SemaphoreType.DMA((1,))],
        compiler_params=compiler_params(),
        cost_estimate=cost(5),
        name="forward0",
    )(shifts, initial, gain, w_qkv, w_out, east, west)


def forward1(shifts, before, noise, east, gain, noise_scale, w_qkv, w_out):
    return pl.pallas_call(
        forward1_kernel,
        out_shape=shapes([((SENT_ROWS, C), BF16), ((ROWS, C), F32), ((2, ROWS, C), F32)] + saved(2)),
        in_specs=[hbm()] + [vmem()] * 7,
        out_specs=[vmem()] * 7,
        scratch_shapes=shifts_buffers()
        + buffers(
            [
                ((LAT, 24, C), F32),
                ((ROWS, C), F32),
                ((ROWS, C), BF16),
                ((ROWS, C), BF16),
            ]
        )
        + [pltpu.SemaphoreType.DMA((1,))],
        compiler_params=compiler_params(),
        cost_estimate=cost(4),
        name="forward1",
    )(shifts, noise, gain, noise_scale, w_qkv, w_out, before, east)


def prepare_kernel(w_qkv_hbm, w_out_hbm, w_qkv, w_out, w_qkv_t, w_out_t, sems):
    copies = start_copies(sems, 0, column_parts(w_qkv_hbm, w_qkv, 6))
    copies += start_copies(sems, 6, column_parts(w_out_hbm, w_out, 2))
    for part in range(8):
        copies[part].wait()
        held, turned = (w_qkv, w_qkv_t) if part < 6 else (w_out, w_out_t)
        at = part % 6 * 512
        turned[at : at + 512, :] = held[:, at : at + 512].T


def prepare(w_qkv, w_out):
    return pl.pallas_call(
        prepare_kernel,
        out_shape=shapes(WEIGHTS + [((3 * C, C), BF16), ((C, C), BF16)]),
        in_specs=[hbm()] * 2,
        out_specs=[vmem()] * 4,
        scratch_shapes=[pltpu.SemaphoreType.DMA((8,))],
        compiler_params=compiler_params(),
        cost_estimate=cost(8),
        name="prepare",
    )(w_qkv, w_out)


def borders_kernel(
    initial_hbm,
    noise_hbm,
    target_hbm,
    east,
    west,
    initial,
    noise,
    target,
    sems,
):
    copies = start_copies(
        sems,
        0,
        [
            (initial_hbm.at[pl.ds(0, 4)], initial.at[pl.ds(0, 4)]),
            (initial_hbm.at[pl.ds(4, 4)], initial.at[pl.ds(4, 4)]),
            (noise_hbm.at[0], noise.at[0]),
            (noise_hbm.at[1], noise.at[1]),
            (target_hbm.at[pl.ds(0, 4)], target.at[pl.ds(0, 4)]),
            (target_hbm.at[pl.ds(4, 4)], target.at[pl.ds(4, 4)]),
        ],
    )

    def rows(held, first, columns):
        return [held[row].astype(F32)[first : first + columns] for row in range(LAT)]

    wait_all(copies[:2])
    spare = jnp.zeros((EAST_ROWS - EAST_INITIAL - INITIAL_ROWS, C), F32)
    east[EAST_INITIAL:, :] = jnp.concatenate(rows(initial, 0, 15) + [spare]).astype(BF16)
    west[...] = jnp.concatenate(rows(initial, WIN, WIN)).astype(BF16)
    wait_all(copies[2:4])
    east[: 2 * NOISE_ROWS, :] = jnp.concatenate(
        rows(noise.at[0], 0, 7) + rows(noise.at[1], 0, 7)
    ).astype(BF16)
    wait_all(copies[4:])
    mine = quarter(member_index())
    part = jnp.concatenate([target[row, 0:WIN, mine] for row in range(LAT)])
    for at in range(4):
        east[2 * NOISE_ROWS : EAST_INITIAL, at * QUARTER : (at + 1) * QUARTER] = part[
            at * PART_ROWS : (at + 1) * PART_ROWS
        ].astype(BF16)


def borders(initial, noise, target):
    return pl.pallas_call(
        borders_kernel,
        out_shape=shapes(
            [
                ((EAST_ROWS, C), BF16),
                ((TOK, C), BF16),
                ((LAT, 16, C), F32),
                ((2, LAT, 16, C), BF16),
                ((LAT, 16, C), F32),
            ]
        ),
        in_specs=[hbm()] * 3,
        out_specs=[vmem()] * 5,
        scratch_shapes=[pltpu.SemaphoreType.DMA((6,))],
        compiler_params=pltpu.CompilerParams(vmem_limit_bytes=52 * 1024 * 1024),
        cost_estimate=cost(2),
        name="borders",
    )(initial, noise, target)


def attend_back(windows, d_mixed, d_packed):
    masks = head_masks()

    def group(at, _):
        for window, (packed, weights_ref) in enumerate(windows):
            rows = slice(window * TOK, (window + 1) * TOK)
            here = lanes(at * LANES, LANES)
            queries = packed[:, here]
            keys = packed[:, lanes(C + at * LANES, LANES)]
            values = packed[:, lanes(2 * C + at * LANES, LANES)]
            d_mixed_blocks = by_head(d_mixed[rows, here], masks)
            weights = weights_ref[at]
            d_weights = dot_nt(values, d_mixed_blocks)
            d_values = dot(weights, d_mixed_blocks)
            probs = weights.astype(F32)
            centred = d_weights - jnp.sum(d_weights * probs, axis=0, keepdims=True)
            d_scores = (probs * centred * SCALE).astype(BF16)
            d_keys = dot(d_scores, by_head(queries, masks))
            d_queries = fold_heads(dot_tn(d_scores, keys), masks)
            d_packed[rows, here] = d_queries.astype(BF16)
            d_packed[rows, lanes(C + at * LANES, LANES)] = d_keys.astype(BF16)
            d_packed[rows, lanes(2 * C + at * LANES, LANES)] = d_values.astype(BF16)
        return 0

    lax.fori_loop(0, GROUPS, group, 0, unroll=GROUPS)


def saved_window(window, packed, weights, scaled, spread):
    rows = pl.ds(pl.multiple_of(window * TOK, TOK), TOK)
    groups = pl.ds(window * GROUPS, GROUPS)
    return packed.at[rows], weights.at[groups], scaled.at[rows], spread.at[rows]


def slope(difference):
    return difference * lax.rsqrt(difference * difference + SMOOTH * SMOOTH)


def step_back(d_next, windows, w_qkv_t, w_out_t, d_mixed, d_packed, d_normed):
    d_branch = d_next[...].astype(BF16)
    for part in range(4):
        at = slice(part * 256, (part + 1) * 256)
        d_mixed[:, at] = dot(d_branch, w_out_t[:, at]).astype(BF16)
    attend_back([window[:2] for window in windows], d_mixed, d_packed)
    for part in range(4):
        at = slice(part * 256, (part + 1) * 256)
        d_normed[:, at] = dot(d_packed[...], w_qkv_t[:, at])


def norm_back(at, d_next, windows, d_normed, gain):
    rows = slice(at, at + 32)
    _, _, scaled_ref, spread_ref = windows[at // TOK]
    inside = slice(at % TOK, at % TOK + 32)
    scaled = scaled_ref[inside, :].astype(F32)
    d_here = d_normed[rows, :]
    d_hat = d_here * gain
    spread = spread_ref[inside, 0:1]
    d_fields = spread * (
        d_hat
        - jnp.mean(d_hat, axis=-1, keepdims=True)
        - scaled * jnp.mean(d_hat * scaled, axis=-1, keepdims=True)
    )
    return d_next[rows, :] + d_fields, eight_rows(d_here * scaled)


def eight_rows(value):
    out = value[0:8]
    for at in range(8, value.shape[0], 8):
        out = out + value[at : at + 8]
    return out


def backward1_kernel(
    shifts_hbm,
    final,
    near,
    far,
    far_near,
    target,
    gain,
    noise,
    packed,
    weights,
    scaled,
    spread,
    w_out_t,
    w_qkv_t,
    sent,
    d_out,
    sent_out,
    head_out,
    gain_out,
    scale_out,
    shifts,
    ext,
    d_next,
    d_mixed,
    d_packed,
    d_normed,
    sems,
):
    small = start_copies(sems, 0, [(shifts_hbm, shifts)])
    me = member_index()
    for other_bits, held in enumerate((sent, near, far, far_near)):
        theirs = quarter(me ^ other_bits)
        part = held[ROWS:SENT_ROWS, :].astype(F32)
        for at in range(4):
            d_next[at * PART_ROWS : (at + 1) * PART_ROWS, theirs] = part[
                :, at * QUARTER : (at + 1) * QUARTER
            ]
    fill(ext, target, d_next[0:TOK, :], 0)
    wait_all(small)
    for row in range(LAT):
        part = frame(ext, row, shifts[1, 1], 16)
        for window in range(2):
            d_normed[window_rows(window, row), :] = part[window * WIN : (window + 1) * WIN]
    scale_total = jnp.zeros((8, C), F32)
    for at in range(0, ROWS, 32):
        rows = slice(at, at + 32)
        here = final[rows, :]
        pairs = (
            slope(here - near[rows, :].astype(F32))
            + slope(here - far[rows, :].astype(F32))
            + slope(here - far_near[rows, :].astype(F32))
        )
        seed = slope(here - d_normed[rows, :]) - pairs * (1.0 / 3.0)
        d_next[rows, :] = seed
        scale_total = scale_total + eight_rows(seed * noise[1, rows, :])
    windows = [saved_window(at, packed, weights, scaled, spread) for at in range(2)]
    step_back(d_next, windows, w_qkv_t, w_out_t, d_mixed, d_packed, d_normed)
    gain_total = jnp.zeros((8, C), F32)
    for at in range(0, ROWS, 32):
        rows = slice(at, at + 32)
        d_here, gain_part = norm_back(at, d_next, windows, d_normed, gain[...])
        d_out[rows, :] = d_here
        sent_out[rows, :] = d_here.astype(BF16)
        if at < TOK:
            head_out[rows, :] = d_here.astype(BF16)
        gain_total = gain_total + gain_part
        scale_total = scale_total + eight_rows(d_here * noise[0, rows, :])
    gain_out[...] = gain_total
    scale_out[...] = scale_total


def inner_window(shifts):
    return jnp.where(shifts[0, 1] >= shifts[1, 1], 1, 2)


def backward0_inner_kernel(
    shifts_hbm,
    gain,
    packed,
    weights,
    scaled,
    spread,
    w_out_t,
    w_qkv_t,
    d_in,
    gain_in,
    d_out,
    gain_out,
    shifts,
    ext,
    d_next,
    d_mixed,
    d_packed,
    d_normed,
    sems,
):
    small = start_copies(sems, 0, [(shifts_hbm, shifts)])
    for row in range(LAT):
        ext[row, 0:8, :] = d_in[row * WIN : (row + 1) * WIN, :]
        ext[row, 8:16, :] = d_in[TOK + row * WIN : TOK + (row + 1) * WIN, :]
    wait_all(small)
    window = inner_window(shifts)
    start = shifts[0, 1] - shifts[1, 1] + (window - 1) * WIN
    for row in range(LAT):
        d_next[row * WIN : (row + 1) * WIN, :] = frame(ext, row, start, WIN)
    windows = [saved_window(window, packed, weights, scaled, spread)]
    step_back(d_next, windows, w_qkv_t, w_out_t, d_mixed, d_packed, d_normed)
    gain_total = gain_in[...]
    for at in range(0, TOK, 32):
        d_here, gain_part = norm_back(at, d_next, windows, d_normed, gain[...])
        d_out[at : at + 32, :] = d_here
        gain_total = gain_total + gain_part
    gain_out[...] = gain_total


def backward0_outer_kernel(
    shifts_hbm,
    gain,
    packed,
    weights,
    scaled,
    spread,
    w_out_t,
    w_qkv_t,
    d_in,
    d_west,
    d_east,
    d_inner,
    gain_in,
    scale_in,
    own_out,
    sums_out,
    shifts,
    ext,
    d_next,
    d_mixed,
    d_packed,
    d_normed,
    sems,
):
    small = start_copies(sems, 0, [(shifts_hbm, shifts)])
    west, east = d_west[...].astype(F32), d_east[...].astype(F32)
    for row in range(LAT):
        here = slice(row * WIN, (row + 1) * WIN)
        there = slice(TOK + row * WIN, TOK + (row + 1) * WIN)
        ext[row, 0:8, :] = west[here]
        ext[row, 8:16, :] = west[there]
        ext[row, 16:24, :] = d_in[here, :]
        ext[row, 24:32, :] = d_in[there, :]
        ext[row, 32:40, :] = east[here]
    wait_all(small)
    lon0 = shifts[0, 1]
    inner = inner_window(shifts)
    picked = [0, 3 - inner]
    start = lon0 - shifts[1, 1] + WIN
    for row in range(LAT):
        for place, window in enumerate(picked):
            d_next[window_rows(place, row), :] = frame(ext, row, start + window * WIN, WIN)
    windows = [saved_window(window, packed, weights, scaled, spread) for window in picked]
    step_back(d_next, windows, w_qkv_t, w_out_t, d_mixed, d_packed, d_normed)
    gain_total = gain_in[...]
    for at in range(0, ROWS, 32):
        d_here, gain_part = norm_back(at, d_next, windows, d_normed, gain[...])
        d_normed[at : at + 32, :] = d_here
        if at >= TOK:
            gain_total = gain_total + gain_part
    sums = [jnp.sum(total, axis=0, keepdims=True) for total in (gain_total, scale_in[...])]
    sums = jnp.concatenate(
        [part[:, at : at + 128] for part in sums for at in range(0, C, 128)]
    ).astype(BF16)
    for copy in range(sums_out.shape[0]):
        sums_out[copy] = sums
    first = inner == 1
    for row in range(LAT):
        done = d_inner[row * WIN : (row + 1) * WIN, :]
        rest = d_normed[window_rows(1, row), :]
        ext[row, 0:8, :] = d_normed[window_rows(0, row), :]
        ext[row, 8:16, :] = jnp.where(first, done, rest)
        ext[row, 16:24, :] = jnp.where(first, rest, done)
        own_out[row] = frame(ext, row, WIN - lon0, 16)


WORK = [
    ((LAT, 24, C), F32),
    ((ROWS, C), F32),
    ((ROWS, C), BF16),
    ((ROWS, 3 * C), BF16),
    ((ROWS, C), F32),
]
SUMS = [((8, C), F32)] * 2


def backward1(shifts, final, sent, others, target, noise, held, gain, w_qkv_t, w_out_t):
    return pl.pallas_call(
        backward1_kernel,
        out_shape=shapes([((ROWS, C), F32), ((ROWS, C), BF16), ((TOK, C), BF16)] + SUMS),
        in_specs=[hbm()] + [vmem()] * 14,
        out_specs=[vmem()] * 5,
        scratch_shapes=shifts_buffers() + buffers(WORK) + [pltpu.SemaphoreType.DMA((1,))],
        compiler_params=compiler_params(),
        cost_estimate=cost(6),
        name="backward1",
    )(shifts, final, *others, target, gain, noise, *held, w_out_t, w_qkv_t, sent)


def backward0_buffers(windows, columns):
    rows = windows * TOK
    return (
        shifts_buffers()
        + buffers(
            [
                ((LAT, columns, C), F32),
                ((rows, C), F32),
                ((rows, C), BF16),
                ((rows, 3 * C), BF16),
                ((rows, C), F32),
            ]
        )
        + [pltpu.SemaphoreType.DMA((1,))]
    )


def backward0_inner(shifts, d_in, held, gain, gain_in, w_qkv_t, w_out_t):
    return pl.pallas_call(
        backward0_inner_kernel,
        out_shape=shapes([((TOK, C), F32), ((8, C), F32)]),
        in_specs=[hbm()] + [vmem()] * 9,
        out_specs=[vmem()] * 2,
        scratch_shapes=backward0_buffers(1, 16),
        compiler_params=compiler_params(),
        cost_estimate=cost(4),
        name="backward0_inner",
    )(shifts, gain, *held, w_out_t, w_qkv_t, d_in, gain_in)


def backward0_outer(copies, shifts, d_parts, held, gain, sums_in, w_qkv_t, w_out_t):
    return pl.pallas_call(
        backward0_outer_kernel,
        out_shape=shapes([((LAT, 16, C), F32), ((copies, 16, 128), BF16)]),
        in_specs=[hbm()] + [vmem()] * 13,
        out_specs=[vmem()] * 2,
        scratch_shapes=backward0_buffers(2, 40),
        compiler_params=compiler_params(),
        cost_estimate=cost(5),
        name="backward0_outer",
    )(shifts, gain, *held, w_out_t, w_qkv_t, *d_parts, *sums_in)


MEMBER = ("pair", "core")
TILE = ("far", "row", "half")


def along(value, steps):
    count = lax.axis_size(TILE)
    return lax.ppermute(value, TILE, [(at, (at + steps) % count) for at in range(count)])


def other(value, axis):
    return lax.ppermute(value, axis, [(0, 1), (1, 0)])


def total_over(copies, axes):
    return jnp.sum(lax.all_to_all(copies, axes, 0, 0).astype(F32), axis=0)


def local(initial, target, noise, w_qkv, w_out, gain, noise_scale, shifts):
    initial, noise = initial[0], noise[:, 0]
    gain_row, scale_row = gain[None], noise_scale[None]
    east, west, initial, noise, target = borders(initial, noise, target)
    east, west = along(east, -1), along(west, 1)
    prepared = prepare(w_qkv, w_out)
    east, west, prepared = lax.optimization_barrier((east, west, prepared))
    here, here_t = prepared[:2], prepared[2:]
    before, *saved0 = forward0(shifts, initial, east, west, gain_row, *here)
    sent, final, noise_here, *saved1 = forward1(
        shifts, before, noise, east, gain_row, scale_row, *here
    )
    far = other(sent, "pair")
    near = other(sent, "core")
    far_near = other(far, "core")
    d_one, d_sent, head, gain_part, scale_part = backward1(
        shifts,
        final,
        sent,
        (near, far, far_near),
        target,
        noise_here,
        saved1,
        gain_row,
        *here_t,
    )
    d_east, d_west = along(head, -1), along(d_sent, 1)
    d_inner, gain_part = backward0_inner(shifts, d_one, saved0, gain_row, gain_part, *here_t)
    near_axes = MEMBER + TILE[1:]
    state_grad, sums = backward0_outer(
        lax.axis_size(near_axes),
        shifts,
        (d_one, d_west, d_east, d_inner),
        saved0,
        gain_row,
        (gain_part, scale_part),
        *here_t,
    )
    sums = total_over(sums, near_axes).astype(BF16)
    sums = jnp.broadcast_to(sums[None], (lax.axis_size(TILE[0]),) + sums.shape)
    sums = total_over(sums, TILE[0]).reshape(2, C)
    members = lax.axis_size(MEMBER)
    factor = (members * LAT * initial.shape[1] * lax.axis_size(TILE)) ** (-0.5)
    return (state_grad[None], sums[0] * factor, sums[1] * factor)


def solution(mesh):
    members, tiles = mesh.devices.shape
    fine = Mesh(mesh.devices.reshape(members // 2, 2, tiles // 8, 4, 2), MEMBER + TILE)
    in_specs = (
        P(MEMBER, None, TILE, None),
        P(None, TILE, None),
        P(None, MEMBER, None, TILE, None),
        P(),
        P(),
        P(),
        P(),
        P(),
    )
    out_specs = (P(MEMBER, None, TILE, None), P(), P())
    return jax.shard_map(local, mesh=fine, in_specs=in_specs, out_specs=out_specs, check_vma=False)
```

```python
import functools

import jax
import jax.numpy as jnp
from jax import lax
from jax.experimental import pallas as pl
from jax.experimental.pallas import tpu as pltpu
from jax.sharding import Mesh
from jax.sharding import PartitionSpec as P

C = 1024
HEAD = 32
WIN = 8
LAT = 8
TOK = LAT * WIN
GROUP = 4
LANES = GROUP * HEAD
GROUPS = C // LANES
SPAN = GROUP * TOK
SCALE = HEAD ** (-0.5)
SMOOTH = 0.25
F32 = jnp.float32
BF16 = jnp.bfloat16
VMEM_LIMIT = 14 * 1024 * 1024


def dot(left, right):
    return lax.dot_general(left, right, (((1,), (0,)), ((), ())), preferred_element_type=F32)


def dot_nt(left, right):
    return lax.dot_general(left, right, (((1,), (1,)), ((), ())), preferred_element_type=F32)


def dot_tn(left, right):
    return lax.dot_general(left, right, (((0,), (0,)), ((), ())), preferred_element_type=F32)


def head_masks():
    lane = lax.broadcasted_iota(jnp.int32, (TOK, LANES), 1) // HEAD
    return [lane == head for head in range(GROUP)]


def head_blocks():
    block = lax.broadcasted_iota(jnp.int32, (SPAN, LANES), 0) // TOK
    lane = lax.broadcasted_iota(jnp.int32, (SPAN, LANES), 1) // HEAD
    return jnp.where(block == lane, 1.0, 0.0).astype(BF16)


def by_head(value, blocks):
    return jnp.concatenate([value] * GROUP, axis=0) * blocks


def fold_heads(stacked, masks):
    out = stacked[:TOK]
    for head in range(1, GROUP):
        out = jnp.where(masks[head], stacked[head * TOK : (head + 1) * TOK], out)
    return out


def lat_mask(lat_shift):
    key_lat = lax.broadcasted_iota(jnp.int32, (TOK, SPAN), 0) // WIN
    query_lat = (lax.broadcasted_iota(jnp.int32, (TOK, SPAN), 1) % TOK) // WIN
    return (key_lat < lat_shift) == (query_lat < lat_shift)


def lanes(start, size):
    return pl.ds(pl.multiple_of(start, 128), size)


def fill(ext, own_ref, side, start):
    columns = side.shape[0] // LAT
    for row in range(LAT):
        ext[row, start : start + 16, :] = own_ref[row].astype(F32)
        ext[row, start + 16 : start + 16 + columns, :] = side[
            row * columns : (row + 1) * columns
        ]


NOISE_ROWS = LAT * 7
PART_ROWS = TOK // 4
EAST_INITIAL = 2 * NOISE_ROWS + PART_ROWS
EAST_ROWS = EAST_INITIAL + LAT * 14
SENT_ROWS = 2 * TOK + PART_ROWS
QUARTER = C // 4
TO_EAST, TO_WEST = 14, 6


def member_index():
    return lax.axis_index("pair") * 2 + lax.axis_index("core")


def quarter(member):
    return pl.ds(pl.multiple_of(member * QUARTER, QUARTER), QUARTER)


def frame(ext, row, start, columns):
    held = ext.shape[1]
    return pltpu.roll(ext[row], lax.rem(held - start, held), 0)[:columns]


def frame_of_eight(ext, row, start):
    base = pl.multiple_of(lax.div(start, 8) * 8, 8)
    return pltpu.roll(ext[row, pl.ds(base, 16), :], lax.rem(16 - lax.rem(start, 8), 16), 0)[:8]


def norm_rows(x_ref, rows, gain, normed_ref, scaled_ref, spread_ref, saved):
    for at in range(0, rows, 32):
        x = x_ref[at : at + 32, :]
        centre = jnp.mean(x, axis=-1, keepdims=True)
        offset = x - centre
        spread = lax.rsqrt(jnp.mean(offset * offset, axis=-1, keepdims=True) + 1e-05)
        scaled = offset * spread
        normed_ref[at : at + 32, :] = (scaled * gain).astype(BF16)
        if at < saved:
            scaled_ref[at : at + 32, :] = scaled.astype(BF16)
            spread_ref[at : at + 32, :] = jnp.broadcast_to(spread, (32, 128))


def attend(windows, packed_ref, weights_ref, mixed_ref, lat_shift, saved):
    masks, blocks = head_masks(), head_blocks()
    allowed = lat_mask(lat_shift)

    def group(at, _):
        for window in range(windows):
            rows = slice(window * TOK, (window + 1) * TOK)
            queries = packed_ref[rows, lanes(at * LANES, LANES)]
            keys = packed_ref[rows, lanes(C + at * LANES, LANES)]
            values = packed_ref[rows, lanes(2 * C + at * LANES, LANES)]
            scores = dot_nt(keys, by_head(queries, blocks))
            scores = jnp.where(allowed, scores, -1e9 / SCALE)
            highest = jnp.max(scores, axis=0, keepdims=True)
            raised = jnp.exp((scores - highest) * SCALE)
            total = jnp.sum(raised, axis=0, keepdims=True)
            weights = (raised * (1.0 / total)).astype(BF16)
            if window < saved:
                weights_ref[window * GROUPS + at] = weights
            mixed = fold_heads(dot_tn(weights, values), masks)
            mixed_ref[rows, lanes(at * LANES, LANES)] = mixed.astype(BF16)
        return 0

    lax.fori_loop(0, GROUPS, group, 0, unroll=GROUPS)


def window_rows(window, row):
    start = window * TOK + row * WIN
    return slice(start, start + WIN)


def start_copies(sems, first, pairs):
    copies = []
    for at, (source, destination) in enumerate(pairs):
        copy = pltpu.make_async_copy(source, destination, sems.at[first + at])
        copy.start()
        copies.append(copy)
    return copies


def wait_all(copies):
    for copy in copies:
        copy.wait()


def column_parts(source, destination, parts):
    width = source.shape[1] // parts
    return [
        (source.at[:, pl.ds(at * width, width)], destination.at[:, pl.ds(at * width, width)])
        for at in range(parts)
    ]


def forward0_kernel(
    shifts_hbm,
    initial,
    gain,
    w_qkv,
    w_out,
    east,
    west,
    following_out,
    packed_out,
    weights_out,
    scaled_out,
    spread_out,
    shifts,
    ext,
    state,
    normed,
    packed,
    mixed,
    sems,
):
    small = start_copies(sems, 0, [(shifts_hbm, shifts)])
    fill(ext, initial, east[EAST_INITIAL:, :].astype(F32), WIN)
    ext[:, 38:40, :] = jnp.zeros((LAT, 2, C), F32)
    before = west[...].astype(F32)
    for row in range(LAT):
        ext[row, 0:WIN, :] = before[row * WIN : (row + 1) * WIN]
    wait_all(small)
    lat_shift = shifts[0, 0]
    for row in range(LAT):
        part = frame(ext, row, shifts[0, 1], 32)
        for window in range(4):
            state[window_rows(window, row), :] = part[window * WIN : (window + 1) * WIN]
    norm_rows(state, 4 * TOK, gain[...], normed, scaled_out, spread_out, 3 * TOK)
    for part in range(6):
        at = slice(part * 512, (part + 1) * 512)
        packed[:, at] = dot(normed[...], w_qkv[:, at]).astype(BF16)
    packed_out[...] = packed[: 3 * TOK, :]
    attend(4, packed, weights_out, mixed, lat_shift, 3)
    for part in range(4):
        at = slice(part * 256, (part + 1) * 256)
        following = state[:, at] + dot(mixed[...], w_out[:, at])
        for row in range(LAT):
            for window in range(4):
                following_out[row, window * WIN : (window + 1) * WIN, at] = following[
                    window_rows(window, row)
                ]


def forward1_kernel(
    shifts_hbm,
    noise,
    gain,
    noise_scale,
    w_qkv,
    w_out,
    before,
    east,
    sent_out,
    final,
    noise_here,
    packed,
    weights,
    scaled,
    spread,
    shifts,
    ext,
    state,
    normed,
    mixed,
    sems,
):
    small = start_copies(sems, 0, [(shifts_hbm, shifts)])
    side = east[: 2 * NOISE_ROWS, :].astype(F32)
    fill(ext, noise.at[0], side[:NOISE_ROWS], 0)
    wait_all(small)
    lat_shift, lon1 = shifts[1, 0], shifts[1, 1]
    scale = noise_scale[...]
    for row in range(LAT):
        part = frame(ext, row, lon1, 16)
        fields = frame(before, row, lon1 - shifts[0, 1] + WIN, 16)
        for window in range(2):
            rows = window_rows(window, row)
            here = part[window * WIN : (window + 1) * WIN]
            state[rows, :] = fields[window * WIN : (window + 1) * WIN] + scale * here
            noise_here[0, rows, :] = here
    fill(ext, noise.at[1], side[NOISE_ROWS:], 0)
    for row in range(LAT):
        part = frame(ext, row, lon1, 16)
        for window in range(2):
            rows = window_rows(window, row)
            here = part[window * WIN : (window + 1) * WIN]
            final[rows, :] = state[rows, :] + scale * here
            noise_here[1, rows, :] = here
    norm_rows(state, 2 * TOK, gain[...], normed, scaled, spread, 2 * TOK)
    for part in range(6):
        at = slice(part * 512, (part + 1) * 512)
        packed[:, at] = dot(normed[...], w_qkv[:, at]).astype(BF16)
    attend(2, packed, weights, mixed, lat_shift, 2)
    for part in range(4):
        at = slice(part * 256, (part + 1) * 256)
        last = final[:, at] + dot(mixed[...], w_out[:, at])
        final[:, at] = last
        sent_out[0:ROWS, at] = last.astype(BF16)
    sent_out[ROWS:SENT_ROWS, :] = east[2 * NOISE_ROWS : EAST_INITIAL, :]


def vmem():
    return pl.BlockSpec(memory_space=pltpu.VMEM)


def hbm():
    return pl.BlockSpec(memory_space=pltpu.HBM)


def cost(microseconds):
    return pl.CostEstimate(
        flops=0, bytes_accessed=int(microseconds * 3_500_000), transcendentals=0
    )


def compiler_params():
    return pltpu.CompilerParams(vmem_limit_bytes=VMEM_LIMIT)


ROWS = 2 * TOK


def saved(windows):
    return [
        ((windows * TOK, 3 * C), BF16),
        ((windows * GROUPS, TOK, SPAN), BF16),
        ((windows * TOK, C), BF16),
        ((windows * TOK, 128), F32),
    ]


def shapes(entries):
    return [jax.ShapeDtypeStruct(shape, dtype) for shape, dtype in entries]


def buffers(entries):
    return [pltpu.VMEM(shape, dtype) for shape, dtype in entries]


WEIGHTS = [((C, 3 * C), BF16), ((C, C), BF16)]


def shifts_buffers():
    return [pltpu.SMEM((2, 2), jnp.int32)]


def forward0(shifts, initial, east, west, gain, w_qkv, w_out):
    rows = 4 * TOK
    return pl.pallas_call(
        forward0_kernel,
        out_shape=shapes([((LAT, 32, C), F32)] + saved(3)),
        in_specs=[hbm()] + [vmem()] * 6,
        out_specs=[vmem()] * 5,
        scratch_shapes=shifts_buffers()
        + buffers(
            [
                ((LAT, 40, C), F32),
                ((rows, C), F32),
                ((rows, C), BF16),
                ((rows, 3 * C), BF16),
                ((rows, C), BF16),
            ]
        )
        + [pltpu.SemaphoreType.DMA((1,))],
        compiler_params=compiler_params(),
        cost_estimate=cost(5),
        name="forward0",
    )(shifts, initial, gain, w_qkv, w_out, east, west)


def forward1(shifts, before, noise, east, gain, noise_scale, w_qkv, w_out):
    return pl.pallas_call(
        forward1_kernel,
        out_shape=shapes([((SENT_ROWS, C), BF16), ((ROWS, C), F32), ((2, ROWS, C), F32)] + saved(2)),
        in_specs=[hbm()] + [vmem()] * 7,
        out_specs=[vmem()] * 7,
        scratch_shapes=shifts_buffers()
        + buffers(
            [
                ((LAT, 24, C), F32),
                ((ROWS, C), F32),
                ((ROWS, C), BF16),
                ((ROWS, C), BF16),
            ]
        )
        + [pltpu.SemaphoreType.DMA((1,))],
        compiler_params=compiler_params(),
        cost_estimate=cost(4),
        name="forward1",
    )(shifts, noise, gain, noise_scale, w_qkv, w_out, before, east)


def prepare_kernel(w_qkv_hbm, w_out_hbm, w_qkv, w_out, w_qkv_t, w_out_t, sems):
    copies = start_copies(sems, 0, column_parts(w_qkv_hbm, w_qkv, 6))
    copies += start_copies(sems, 6, column_parts(w_out_hbm, w_out, 2))
    for part in range(8):
        copies[part].wait()
        held, turned = (w_qkv, w_qkv_t) if part < 6 else (w_out, w_out_t)
        at = part % 6 * 512
        turned[at : at + 512, :] = held[:, at : at + 512].T


def prepare(w_qkv, w_out):
    return pl.pallas_call(
        prepare_kernel,
        out_shape=shapes(WEIGHTS + [((3 * C, C), BF16), ((C, C), BF16)]),
        in_specs=[hbm()] * 2,
        out_specs=[vmem()] * 4,
        scratch_shapes=[pltpu.SemaphoreType.DMA((8,))],
        compiler_params=compiler_params(),
        cost_estimate=cost(8),
        name="prepare",
    )(w_qkv, w_out)


def borders_kernel(
    initial_hbm,
    noise_hbm,
    target_hbm,
    east,
    west,
    initial,
    noise,
    target,
    sems,
):
    copies = start_copies(
        sems,
        0,
        [
            (initial_hbm.at[pl.ds(0, 4)], initial.at[pl.ds(0, 4)]),
            (initial_hbm.at[pl.ds(4, 4)], initial.at[pl.ds(4, 4)]),
            (noise_hbm.at[0], noise.at[0]),
            (noise_hbm.at[1], noise.at[1]),
            (target_hbm.at[pl.ds(0, 4)], target.at[pl.ds(0, 4)]),
            (target_hbm.at[pl.ds(4, 4)], target.at[pl.ds(4, 4)]),
        ],
    )

    def rows(held, first, columns):
        return [held[row].astype(F32)[first : first + columns] for row in range(LAT)]

    wait_all(copies[:2])
    east[EAST_INITIAL:, :] = jnp.concatenate(rows(initial, 0, 14)).astype(BF16)
    west[...] = jnp.concatenate(rows(initial, WIN, WIN)).astype(BF16)
    wait_all(copies[2:4])
    east[: 2 * NOISE_ROWS, :] = jnp.concatenate(
        rows(noise.at[0], 0, 7) + rows(noise.at[1], 0, 7)
    ).astype(BF16)
    wait_all(copies[4:])
    mine = quarter(member_index())
    part = jnp.concatenate([target[row, 0:WIN, mine] for row in range(LAT)])
    for at in range(4):
        east[2 * NOISE_ROWS : EAST_INITIAL, at * QUARTER : (at + 1) * QUARTER] = part[
            at * PART_ROWS : (at + 1) * PART_ROWS
        ].astype(BF16)


def borders(initial, noise, target):
    return pl.pallas_call(
        borders_kernel,
        out_shape=shapes(
            [
                ((EAST_ROWS, C), BF16),
                ((TOK, C), BF16),
                ((LAT, 16, C), F32),
                ((2, LAT, 16, C), BF16),
                ((LAT, 16, C), F32),
            ]
        ),
        in_specs=[hbm()] * 3,
        out_specs=[vmem()] * 5,
        scratch_shapes=[pltpu.SemaphoreType.DMA((6,))],
        compiler_params=pltpu.CompilerParams(vmem_limit_bytes=52 * 1024 * 1024),
        cost_estimate=cost(2),
        name="borders",
    )(initial, noise, target)


def attend_back(windows, d_mixed, d_packed):
    masks, blocks = head_masks(), head_blocks()

    def group(at, _):
        for window, (packed, weights_ref) in enumerate(windows):
            rows = slice(window * TOK, (window + 1) * TOK)
            here = lanes(at * LANES, LANES)
            queries = packed[:, here]
            keys = packed[:, lanes(C + at * LANES, LANES)]
            values = packed[:, lanes(2 * C + at * LANES, LANES)]
            d_mixed_blocks = by_head(d_mixed[rows, here], blocks)
            weights = weights_ref[at]
            d_weights = dot_nt(values, d_mixed_blocks)
            d_values = dot(weights, d_mixed_blocks)
            probs = weights.astype(F32)
            centred = d_weights - jnp.sum(d_weights * probs, axis=0, keepdims=True)
            d_scores = (probs * centred * SCALE).astype(BF16)
            d_keys = dot(d_scores, by_head(queries, blocks))
            d_queries = fold_heads(dot_tn(d_scores, keys), masks)
            d_packed[rows, here] = d_queries.astype(BF16)
            d_packed[rows, lanes(C + at * LANES, LANES)] = d_keys.astype(BF16)
            d_packed[rows, lanes(2 * C + at * LANES, LANES)] = d_values.astype(BF16)
        return 0

    lax.fori_loop(0, GROUPS, group, 0, unroll=GROUPS)


def saved_window(window, packed, weights, scaled, spread):
    rows = pl.ds(pl.multiple_of(window * TOK, TOK), TOK)
    groups = pl.ds(window * GROUPS, GROUPS)
    return packed.at[rows], weights.at[groups], scaled.at[rows], spread.at[rows]


def slope(difference):
    return difference * lax.rsqrt(difference * difference + SMOOTH * SMOOTH)


def step_back(d_next, windows, w_qkv_t, w_out_t, d_mixed, d_packed, d_normed):
    d_branch = d_next[...].astype(BF16)
    for part in range(4):
        at = slice(part * 256, (part + 1) * 256)
        d_mixed[:, at] = dot(d_branch, w_out_t[:, at]).astype(BF16)
    attend_back([window[:2] for window in windows], d_mixed, d_packed)
    for part in range(4):
        at = slice(part * 256, (part + 1) * 256)
        d_normed[:, at] = dot(d_packed[...], w_qkv_t[:, at])


def norm_back(at, d_next, windows, d_normed, gain):
    rows = slice(at, at + 32)
    _, _, scaled_ref, spread_ref = windows[at // TOK]
    inside = slice(at % TOK, at % TOK + 32)
    scaled = scaled_ref[inside, :].astype(F32)
    d_here = d_normed[rows, :]
    d_hat = d_here * gain
    spread = spread_ref[inside, 0:1]
    d_fields = spread * (
        d_hat
        - jnp.mean(d_hat, axis=-1, keepdims=True)
        - scaled * jnp.mean(d_hat * scaled, axis=-1, keepdims=True)
    )
    return d_next[rows, :] + d_fields, eight_rows(d_here * scaled)


def eight_rows(value):
    out = value[0:8]
    for at in range(8, value.shape[0], 8):
        out = out + value[at : at + 8]
    return out


def backward1_kernel(
    shifts_hbm,
    final,
    near,
    far,
    far_near,
    target,
    gain,
    noise,
    packed,
    weights,
    scaled,
    spread,
    w_out_t,
    w_qkv_t,
    sent,
    d_out,
    sent_out,
    head_out,
    gain_out,
    scale_out,
    shifts,
    ext,
    d_next,
    d_mixed,
    d_packed,
    d_normed,
    sems,
):
    small = start_copies(sems, 0, [(shifts_hbm, shifts)])
    me = member_index()
    for other_bits, held in enumerate((sent, near, far, far_near)):
        theirs = quarter(me ^ other_bits)
        part = held[ROWS:SENT_ROWS, :].astype(F32)
        for at in range(4):
            d_next[at * PART_ROWS : (at + 1) * PART_ROWS, theirs] = part[
                :, at * QUARTER : (at + 1) * QUARTER
            ]
    fill(ext, target, d_next[0:TOK, :], 0)
    wait_all(small)
    for row in range(LAT):
        part = frame(ext, row, shifts[1, 1], 16)
        for window in range(2):
            d_normed[window_rows(window, row), :] = part[window * WIN : (window + 1) * WIN]
    scale_total = jnp.zeros((8, C), F32)
    for at in range(0, ROWS, 32):
        rows = slice(at, at + 32)
        here = final[rows, :]
        pairs = (
            slope(here - near[rows, :].astype(F32))
            + slope(here - far[rows, :].astype(F32))
            + slope(here - far_near[rows, :].astype(F32))
        )
        seed = slope(here - d_normed[rows, :]) - pairs * (1.0 / 3.0)
        d_next[rows, :] = seed
        scale_total = scale_total + eight_rows(seed * noise[1, rows, :])
    windows = [saved_window(at, packed, weights, scaled, spread) for at in range(2)]
    step_back(d_next, windows, w_qkv_t, w_out_t, d_mixed, d_packed, d_normed)
    gain_total = jnp.zeros((8, C), F32)
    for at in range(0, ROWS, 32):
        rows = slice(at, at + 32)
        d_here, gain_part = norm_back(at, d_next, windows, d_normed, gain[...])
        d_out[rows, :] = d_here
        gain_total = gain_total + gain_part
        scale_total = scale_total + eight_rows(d_here * noise[0, rows, :])
    gain_out[...] = gain_total
    scale_out[...] = scale_total
    first = [d_out[window_rows(0, row), :] for row in range(LAT)]
    second = [d_out[window_rows(1, row), :] for row in range(LAT)]
    head_out[...] = jnp.concatenate([part[:TO_WEST] for part in first]).astype(BF16)
    skipped = 16 - TO_EAST
    sent_out[...] = jnp.concatenate(
        [part for row in range(LAT) for part in (first[row][skipped:], second[row])]
    ).astype(BF16)


def inner_window(shifts):
    return jnp.where(shifts[0, 1] >= shifts[1, 1], 1, 2)


def backward0_inner_kernel(
    shifts_hbm,
    gain,
    packed,
    weights,
    scaled,
    spread,
    w_out_t,
    w_qkv_t,
    d_in,
    gain_in,
    d_out,
    gain_out,
    shifts,
    ext,
    d_next,
    d_mixed,
    d_packed,
    d_normed,
    sems,
):
    small = start_copies(sems, 0, [(shifts_hbm, shifts)])
    for row in range(LAT):
        ext[row, 0:8, :] = d_in[row * WIN : (row + 1) * WIN, :]
        ext[row, 8:16, :] = d_in[TOK + row * WIN : TOK + (row + 1) * WIN, :]
    wait_all(small)
    window = inner_window(shifts)
    start = shifts[0, 1] - shifts[1, 1] + (window - 1) * WIN
    for row in range(LAT):
        d_next[row * WIN : (row + 1) * WIN, :] = frame(ext, row, start, WIN)
    windows = [saved_window(window, packed, weights, scaled, spread)]
    step_back(d_next, windows, w_qkv_t, w_out_t, d_mixed, d_packed, d_normed)
    gain_total = gain_in[...]
    for at in range(0, TOK, 32):
        d_here, gain_part = norm_back(at, d_next, windows, d_normed, gain[...])
        d_out[at : at + 32, :] = d_here
        gain_total = gain_total + gain_part
    gain_out[...] = gain_total


def backward0_outer_kernel(
    shifts_hbm,
    gain,
    packed,
    weights,
    scaled,
    spread,
    w_out_t,
    w_qkv_t,
    d_in,
    d_west,
    d_east,
    d_inner,
    gain_in,
    scale_in,
    own_out,
    sums_out,
    shifts,
    ext,
    d_next,
    d_mixed,
    d_packed,
    d_normed,
    sems,
):
    small = start_copies(sems, 0, [(shifts_hbm, shifts)])
    west, east = d_west[...].astype(F32), d_east[...].astype(F32)
    for row in range(LAT):
        here = slice(row * WIN, (row + 1) * WIN)
        there = slice(TOK + row * WIN, TOK + (row + 1) * WIN)
        ext[row, 16 - TO_EAST : 16, :] = west[row * TO_EAST : (row + 1) * TO_EAST]
        ext[row, 16:24, :] = d_in[here, :]
        ext[row, 24:32, :] = d_in[there, :]
        ext[row, 32 : 32 + TO_WEST, :] = east[row * TO_WEST : (row + 1) * TO_WEST]
    wait_all(small)
    lon0 = shifts[0, 1]
    inner = inner_window(shifts)
    picked = [0, 3 - inner]
    start = lon0 - shifts[1, 1] + WIN
    for row in range(LAT):
        for place, window in enumerate(picked):
            d_next[window_rows(place, row), :] = frame_of_eight(ext, row, start + window * WIN)
    windows = [saved_window(window, packed, weights, scaled, spread) for window in picked]
    step_back(d_next, windows, w_qkv_t, w_out_t, d_mixed, d_packed, d_normed)
    gain_total = gain_in[...]
    for at in range(0, ROWS, 32):
        d_here, gain_part = norm_back(at, d_next, windows, d_normed, gain[...])
        d_normed[at : at + 32, :] = d_here
        if at >= TOK:
            gain_total = gain_total + gain_part
    sums = [jnp.sum(total, axis=0, keepdims=True) for total in (gain_total, scale_in[...])]
    sums = jnp.concatenate(
        [part[:, at : at + 128] for part in sums for at in range(0, C, 128)]
    ).astype(BF16)
    for copy in range(sums_out.shape[0]):
        sums_out[copy] = sums
    first = inner == 1
    for row in range(LAT):
        done = d_inner[row * WIN : (row + 1) * WIN, :]
        rest = d_normed[window_rows(1, row), :]
        ext[row, 0:8, :] = d_normed[window_rows(0, row), :]
        ext[row, 8:16, :] = jnp.where(first, done, rest)
        ext[row, 16:24, :] = jnp.where(first, rest, done)
        own_out[row] = frame(ext, row, WIN - lon0, 16)


WORK = [
    ((LAT, 24, C), F32),
    ((ROWS, C), F32),
    ((ROWS, C), BF16),
    ((ROWS, 3 * C), BF16),
    ((ROWS, C), F32),
]
SUMS = [((8, C), F32)] * 2


def backward1(shifts, final, sent, others, target, noise, held, gain, w_qkv_t, w_out_t):
    return pl.pallas_call(
        backward1_kernel,
        out_shape=shapes(
            [((ROWS, C), F32), ((LAT * TO_EAST, C), BF16), ((LAT * TO_WEST, C), BF16)] + SUMS
        ),
        in_specs=[hbm()] + [vmem()] * 14,
        out_specs=[vmem()] * 5,
        scratch_shapes=shifts_buffers() + buffers(WORK) + [pltpu.SemaphoreType.DMA((1,))],
        compiler_params=compiler_params(),
        cost_estimate=cost(6),
        name="backward1",
    )(shifts, final, *others, target, gain, noise, *held, w_out_t, w_qkv_t, sent)


def backward0_buffers(windows, columns):
    rows = windows * TOK
    return (
        shifts_buffers()
        + buffers(
            [
                ((LAT, columns, C), F32),
                ((rows, C), F32),
                ((rows, C), BF16),
                ((rows, 3 * C), BF16),
                ((rows, C), F32),
            ]
        )
        + [pltpu.SemaphoreType.DMA((1,))]
    )


def backward0_inner(shifts, d_in, held, gain, gain_in, w_qkv_t, w_out_t):
    return pl.pallas_call(
        backward0_inner_kernel,
        out_shape=shapes([((TOK, C), F32), ((8, C), F32)]),
        in_specs=[hbm()] + [vmem()] * 9,
        out_specs=[vmem()] * 2,
        scratch_shapes=backward0_buffers(1, 16),
        compiler_params=compiler_params(),
        cost_estimate=cost(4),
        name="backward0_inner",
    )(shifts, gain, *held, w_out_t, w_qkv_t, d_in, gain_in)


def backward0_outer(copies, shifts, d_parts, held, gain, sums_in, w_qkv_t, w_out_t):
    return pl.pallas_call(
        backward0_outer_kernel,
        out_shape=shapes([((LAT, 16, C), F32), ((copies, 16, 128), BF16)]),
        in_specs=[hbm()] + [vmem()] * 13,
        out_specs=[vmem()] * 2,
        scratch_shapes=backward0_buffers(2, 40),
        compiler_params=compiler_params(),
        cost_estimate=cost(5),
        name="backward0_outer",
    )(shifts, gain, *held, w_out_t, w_qkv_t, *d_parts, *sums_in)


MEMBER = ("pair", "core")
TILE = ("far", "row", "half")


def along(value, steps):
    count = lax.axis_size(TILE)
    return lax.ppermute(value, TILE, [(at, (at + steps) % count) for at in range(count)])


def other(value, axis):
    return lax.ppermute(value, axis, [(0, 1), (1, 0)])


def total_over(copies, axes, groups=None):
    parts = lax.all_to_all(copies, axes, 0, 0, axis_index_groups=groups)
    return jnp.sum(parts.astype(F32), axis=0)


def local(initial, target, noise, w_qkv, w_out, gain, noise_scale, shifts):
    initial, noise = initial[0], noise[:, 0]
    gain_row, scale_row = gain[None], noise_scale[None]
    east, west, initial, noise, target = borders(initial, noise, target)
    east, west = along(east, -1), along(west, 1)
    prepared = prepare(w_qkv, w_out)
    east, west, prepared = lax.optimization_barrier((east, west, prepared))
    here, here_t = prepared[:2], prepared[2:]
    before, *saved0 = forward0(shifts, initial, east, west, gain_row, *here)
    sent, final, noise_here, *saved1 = forward1(
        shifts, before, noise, east, gain_row, scale_row, *here
    )
    far = other(sent, "pair")
    near = other(sent, "core")
    far_near = other(far, "core")
    d_one, d_sent, head, gain_part, scale_part = backward1(
        shifts,
        final,
        sent,
        (near, far, far_near),
        target,
        noise_here,
        saved1,
        gain_row,
        *here_t,
    )
    d_east, d_west = along(head, -1), along(d_sent, 1)
    d_inner, gain_part = backward0_inner(shifts, d_one, saved0, gain_row, gain_part, *here_t)
    near_axes = MEMBER + TILE[1:]
    state_grad, sums = backward0_outer(
        lax.axis_size(near_axes),
        shifts,
        (d_one, d_west, d_east, d_inner),
        saved0,
        gain_row,
        (gain_part, scale_part),
        *here_t,
    )
    sums = total_over(sums, near_axes).astype(BF16)
    count = lax.axis_size(TILE[0])
    sums = jnp.broadcast_to(sums[None], (count,) + sums.shape)
    sums = total_over(sums, TILE[0], [list(range(count))[::-1]]).reshape(2, C)
    members = lax.axis_size(MEMBER)
    factor = (members * LAT * initial.shape[1] * lax.axis_size(TILE)) ** (-0.5)
    return (state_grad[None], sums[0] * factor, sums[1] * factor)


def solution(mesh):
    members, tiles = mesh.devices.shape
    fine = Mesh(mesh.devices.reshape(members // 2, 2, tiles // 8, 4, 2), MEMBER + TILE)
    in_specs = (
        P(MEMBER, None, TILE, None),
        P(None, TILE, None),
        P(None, MEMBER, None, TILE, None),
        P(),
        P(),
        P(),
        P(),
        P(),
    )
    out_specs = (P(MEMBER, None, TILE, None), P(), P())
    return jax.shard_map(local, mesh=fine, in_specs=in_specs, out_specs=out_specs, check_vma=False)
```

```python
import functools

import jax
import jax.numpy as jnp
from jax import lax
from jax.experimental import pallas as pl
from jax.experimental.pallas import tpu as pltpu
from jax.sharding import Mesh
from jax.sharding import PartitionSpec as P

C = 1024
HEAD = 32
WIN = 8
LAT = 8
TOK = LAT * WIN
GROUP = 4
LANES = GROUP * HEAD
GROUPS = C // LANES
SPAN = GROUP * TOK
SCALE = HEAD ** (-0.5)
SMOOTH = 0.25
F32 = jnp.float32
BF16 = jnp.bfloat16
VMEM_LIMIT = 14 * 1024 * 1024


def dot(left, right):
    return lax.dot_general(left, right, (((1,), (0,)), ((), ())), preferred_element_type=F32)


def dot_nt(left, right):
    return lax.dot_general(left, right, (((1,), (1,)), ((), ())), preferred_element_type=F32)


def dot_tn(left, right):
    return lax.dot_general(left, right, (((0,), (0,)), ((), ())), preferred_element_type=F32)


def head_masks():
    lane = lax.broadcasted_iota(jnp.int32, (TOK, LANES), 1) // HEAD
    return [lane == head for head in range(GROUP)]


def head_blocks():
    block = lax.broadcasted_iota(jnp.int32, (SPAN, LANES), 0) // TOK
    lane = lax.broadcasted_iota(jnp.int32, (SPAN, LANES), 1) // HEAD
    return jnp.where(block == lane, 1.0, 0.0).astype(BF16)


def by_head(value, blocks):
    return jnp.concatenate([value] * GROUP, axis=0) * blocks


def fold_heads(stacked, masks):
    out = stacked[:TOK]
    for head in range(1, GROUP):
        out = jnp.where(masks[head], stacked[head * TOK : (head + 1) * TOK], out)
    return out


def lat_mask(lat_shift):
    key_lat = lax.broadcasted_iota(jnp.int32, (TOK, SPAN), 0) // WIN
    query_lat = (lax.broadcasted_iota(jnp.int32, (TOK, SPAN), 1) % TOK) // WIN
    return (key_lat < lat_shift) == (query_lat < lat_shift)


def lanes(start, size):
    return pl.ds(pl.multiple_of(start, 128), size)


def fill(ext, own_ref, side, start):
    columns = side.shape[0] // LAT
    for row in range(LAT):
        ext[row, start : start + 16, :] = own_ref[row].astype(F32)
        ext[row, start + 16 : start + 16 + columns, :] = side[
            row * columns : (row + 1) * columns
        ]


NOISE_ROWS = LAT * 7
PART_ROWS = TOK // 4
EAST_INITIAL = 2 * NOISE_ROWS + PART_ROWS
EAST_ROWS = EAST_INITIAL + LAT * 14
SENT_ROWS = 2 * TOK + PART_ROWS
QUARTER = C // 4
TO_EAST, TO_WEST = 14, 6


def member_index():
    return lax.axis_index("pair") * 2 + lax.axis_index("core")


def quarter(member):
    return pl.ds(pl.multiple_of(member * QUARTER, QUARTER), QUARTER)


def frame(ext, row, start, columns):
    held = ext.shape[1]
    return pltpu.roll(ext[row], lax.rem(held - start, held), 0)[:columns]


def frame_of_eight(ext, row, start):
    base = pl.multiple_of(lax.div(start, 8) * 8, 8)
    return pltpu.roll(ext[row, pl.ds(base, 16), :], lax.rem(16 - lax.rem(start, 8), 16), 0)[:8]


def norm_rows(x_ref, rows, gain, normed_ref, scaled_ref, spread_ref, saved):
    for at in range(0, rows, 32):
        x = x_ref[at : at + 32, :]
        centre = jnp.mean(x, axis=-1, keepdims=True)
        offset = x - centre
        spread = lax.rsqrt(jnp.mean(offset * offset, axis=-1, keepdims=True) + 1e-05)
        scaled = offset * spread
        normed_ref[at : at + 32, :] = (scaled * gain).astype(BF16)
        if at < saved:
            scaled_ref[at : at + 32, :] = scaled.astype(BF16)
            spread_ref[at : at + 32, :] = jnp.broadcast_to(spread, (32, 128))


def attend(windows, packed_ref, weights_ref, mixed_ref, lat_shift, saved):
    masks, blocks = head_masks(), head_blocks()
    allowed = lat_mask(lat_shift)

    def group(at, _):
        for window in range(windows):
            rows = slice(window * TOK, (window + 1) * TOK)
            queries = packed_ref[rows, lanes(at * LANES, LANES)]
            keys = packed_ref[rows, lanes(C + at * LANES, LANES)]
            values = packed_ref[rows, lanes(2 * C + at * LANES, LANES)]
            scores = dot_nt(keys, by_head(queries, blocks))
            scores = jnp.where(allowed, scores, -1e9 / SCALE)
            highest = jnp.max(scores, axis=0, keepdims=True)
            raised = jnp.exp((scores - highest) * SCALE)
            total = jnp.sum(raised, axis=0, keepdims=True)
            weights = (raised * (1.0 / total)).astype(BF16)
            if window < saved:
                weights_ref[window * GROUPS + at] = weights
            mixed = fold_heads(dot_tn(weights, values), masks)
            mixed_ref[rows, lanes(at * LANES, LANES)] = mixed.astype(BF16)
        return 0

    lax.fori_loop(0, GROUPS, group, 0, unroll=GROUPS)


def window_rows(window, row):
    start = window * TOK + row * WIN
    return slice(start, start + WIN)


def start_copies(sems, first, pairs):
    copies = []
    for at, (source, destination) in enumerate(pairs):
        copy = pltpu.make_async_copy(source, destination, sems.at[first + at])
        copy.start()
        copies.append(copy)
    return copies


def wait_all(copies):
    for copy in copies:
        copy.wait()


def column_parts(source, destination, parts):
    width = source.shape[1] // parts
    return [
        (source.at[:, pl.ds(at * width, width)], destination.at[:, pl.ds(at * width, width)])
        for at in range(parts)
    ]


def forward0_kernel(
    shifts_hbm,
    initial,
    gain,
    w_qkv,
    w_out,
    east,
    west,
    following_out,
    packed_out,
    weights_out,
    scaled_out,
    spread_out,
    shifts,
    ext,
    state,
    normed,
    packed,
    mixed,
    sems,
):
    small = start_copies(sems, 0, [(shifts_hbm, shifts)])
    fill(ext, initial, east[EAST_INITIAL:, :].astype(F32), WIN)
    ext[:, 38:40, :] = jnp.zeros((LAT, 2, C), F32)
    before = west[...].astype(F32)
    for row in range(LAT):
        ext[row, 0:WIN, :] = before[row * WIN : (row + 1) * WIN]
    wait_all(small)
    lat_shift = shifts[0, 0]
    for row in range(LAT):
        part = frame(ext, row, shifts[0, 1], 32)
        for window in range(4):
            state[window_rows(window, row), :] = part[window * WIN : (window + 1) * WIN]
    norm_rows(state, 4 * TOK, gain[...], normed, scaled_out, spread_out, 3 * TOK)
    for part in range(6):
        at = slice(part * 512, (part + 1) * 512)
        packed[:, at] = dot(normed[...], w_qkv[:, at]).astype(BF16)
    packed_out[...] = packed[: 3 * TOK, :]
    attend(4, packed, weights_out, mixed, lat_shift, 3)
    for part in range(4):
        at = slice(part * 256, (part + 1) * 256)
        following = state[:, at] + dot(mixed[...], w_out[:, at])
        for row in range(LAT):
            for window in range(4):
                following_out[row, window * WIN : (window + 1) * WIN, at] = following[
                    window_rows(window, row)
                ]


def forward1_kernel(
    shifts_hbm,
    noise,
    gain,
    noise_scale,
    w_qkv,
    w_out,
    before,
    east,
    sent_out,
    final,
    noise_here,
    packed,
    weights,
    scaled,
    spread,
    shifts,
    ext,
    state,
    normed,
    mixed,
    sems,
):
    small = start_copies(sems, 0, [(shifts_hbm, shifts)])
    side = east[: 2 * NOISE_ROWS, :].astype(F32)
    fill(ext, noise.at[0], side[:NOISE_ROWS], 0)
    wait_all(small)
    lat_shift, lon1 = shifts[1, 0], shifts[1, 1]
    scale = noise_scale[...]
    for row in range(LAT):
        part = frame(ext, row, lon1, 16)
        fields = frame(before, row, lon1 - shifts[0, 1] + WIN, 16)
        for window in range(2):
            rows = window_rows(window, row)
            here = part[window * WIN : (window + 1) * WIN]
            state[rows, :] = fields[window * WIN : (window + 1) * WIN] + scale * here
            noise_here[0, rows, :] = here
    fill(ext, noise.at[1], side[NOISE_ROWS:], 0)
    for row in range(LAT):
        part = frame(ext, row, lon1, 16)
        for window in range(2):
            rows = window_rows(window, row)
            here = part[window * WIN : (window + 1) * WIN]
            final[rows, :] = state[rows, :] + scale * here
            noise_here[1, rows, :] = here
    norm_rows(state, 2 * TOK, gain[...], normed, scaled, spread, 2 * TOK)
    for part in range(6):
        at = slice(part * 512, (part + 1) * 512)
        packed[:, at] = dot(normed[...], w_qkv[:, at]).astype(BF16)
    attend(2, packed, weights, mixed, lat_shift, 2)
    for part in range(4):
        at = slice(part * 256, (part + 1) * 256)
        last = final[:, at] + dot(mixed[...], w_out[:, at])
        final[:, at] = last
        sent_out[0:ROWS, at] = last.astype(BF16)
    sent_out[ROWS:SENT_ROWS, :] = east[2 * NOISE_ROWS : EAST_INITIAL, :]


def vmem():
    return pl.BlockSpec(memory_space=pltpu.VMEM)


def hbm():
    return pl.BlockSpec(memory_space=pltpu.HBM)


def cost(microseconds):
    return pl.CostEstimate(
        flops=0, bytes_accessed=int(microseconds * 3_500_000), transcendentals=0
    )


def compiler_params():
    return pltpu.CompilerParams(vmem_limit_bytes=VMEM_LIMIT)


ROWS = 2 * TOK


def saved(windows):
    return [
        ((windows * TOK, 3 * C), BF16),
        ((windows * GROUPS, TOK, SPAN), BF16),
        ((windows * TOK, C), BF16),
        ((windows * TOK, 128), F32),
    ]


def shapes(entries):
    return [jax.ShapeDtypeStruct(shape, dtype) for shape, dtype in entries]


def buffers(entries):
    return [pltpu.VMEM(shape, dtype) for shape, dtype in entries]


WEIGHTS = [((C, 3 * C), BF16), ((C, C), BF16)]


def shifts_buffers():
    return [pltpu.SMEM((2, 2), jnp.int32)]


def forward0(shifts, initial, east, west, gain, w_qkv, w_out):
    rows = 4 * TOK
    return pl.pallas_call(
        forward0_kernel,
        out_shape=shapes([((LAT, 32, C), F32)] + saved(3)),
        in_specs=[hbm()] + [vmem()] * 6,
        out_specs=[vmem()] * 5,
        scratch_shapes=shifts_buffers()
        + buffers(
            [
                ((LAT, 40, C), F32),
                ((rows, C), F32),
                ((rows, C), BF16),
                ((rows, 3 * C), BF16),
                ((rows, C), BF16),
            ]
        )
        + [pltpu.SemaphoreType.DMA((1,))],
        compiler_params=compiler_params(),
        cost_estimate=cost(5),
        name="forward0",
    )(shifts, initial, gain, w_qkv, w_out, east, west)


def forward1(shifts, before, noise, east, gain, noise_scale, w_qkv, w_out):
    return pl.pallas_call(
        forward1_kernel,
        out_shape=shapes([((SENT_ROWS, C), BF16), ((ROWS, C), F32), ((2, ROWS, C), F32)] + saved(2)),
        in_specs=[hbm()] + [vmem()] * 7,
        out_specs=[vmem()] * 7,
        scratch_shapes=shifts_buffers()
        + buffers(
            [
                ((LAT, 24, C), F32),
                ((ROWS, C), F32),
                ((ROWS, C), BF16),
                ((ROWS, C), BF16),
            ]
        )
        + [pltpu.SemaphoreType.DMA((1,))],
        compiler_params=compiler_params(),
        cost_estimate=cost(4),
        name="forward1",
    )(shifts, noise, gain, noise_scale, w_qkv, w_out, before, east)


def prepare_kernel(w_qkv_hbm, w_out_hbm, w_qkv, w_out, w_qkv_t, w_out_t, sems):
    copies = start_copies(sems, 0, column_parts(w_qkv_hbm, w_qkv, 6))
    copies += start_copies(sems, 6, column_parts(w_out_hbm, w_out, 2))
    for part in range(8):
        copies[part].wait()
        held, turned = (w_qkv, w_qkv_t) if part < 6 else (w_out, w_out_t)
        at = part % 6 * 512
        turned[at : at + 512, :] = held[:, at : at + 512].T


def prepare(w_qkv, w_out):
    return pl.pallas_call(
        prepare_kernel,
        out_shape=shapes(WEIGHTS + [((3 * C, C), BF16), ((C, C), BF16)]),
        in_specs=[hbm()] * 2,
        out_specs=[vmem()] * 4,
        scratch_shapes=[pltpu.SemaphoreType.DMA((8,))],
        compiler_params=compiler_params(),
        cost_estimate=cost(8),
        name="prepare",
    )(w_qkv, w_out)


def borders_kernel(
    initial_hbm,
    noise_hbm,
    target_hbm,
    east,
    west,
    initial,
    noise,
    target,
    sems,
):
    copies = start_copies(
        sems,
        0,
        [
            (initial_hbm.at[pl.ds(0, 4)], initial.at[pl.ds(0, 4)]),
            (initial_hbm.at[pl.ds(4, 4)], initial.at[pl.ds(4, 4)]),
            (noise_hbm.at[0], noise.at[0]),
            (noise_hbm.at[1], noise.at[1]),
            (target_hbm.at[pl.ds(0, 4)], target.at[pl.ds(0, 4)]),
            (target_hbm.at[pl.ds(4, 4)], target.at[pl.ds(4, 4)]),
        ],
    )

    def rows(held, first, columns):
        return [held[row].astype(F32)[first : first + columns] for row in range(LAT)]

    wait_all(copies[:2])
    east[EAST_INITIAL:, :] = jnp.concatenate(rows(initial, 0, 14)).astype(BF16)
    west[...] = jnp.concatenate(rows(initial, WIN, WIN)).astype(BF16)
    wait_all(copies[2:4])
    east[: 2 * NOISE_ROWS, :] = jnp.concatenate(
        rows(noise.at[0], 0, 7) + rows(noise.at[1], 0, 7)
    ).astype(BF16)
    wait_all(copies[4:])
    mine = quarter(member_index())
    part = jnp.concatenate([target[row, 0:WIN, mine] for row in range(LAT)])
    for at in range(4):
        east[2 * NOISE_ROWS : EAST_INITIAL, at * QUARTER : (at + 1) * QUARTER] = part[
            at * PART_ROWS : (at + 1) * PART_ROWS
        ].astype(BF16)


def borders(initial, noise, target):
    return pl.pallas_call(
        borders_kernel,
        out_shape=shapes(
            [
                ((EAST_ROWS, C), BF16),
                ((TOK, C), BF16),
                ((LAT, 16, C), F32),
                ((2, LAT, 16, C), BF16),
                ((LAT, 16, C), F32),
            ]
        ),
        in_specs=[hbm()] * 3,
        out_specs=[vmem()] * 5,
        scratch_shapes=[pltpu.SemaphoreType.DMA((6,))],
        compiler_params=pltpu.CompilerParams(vmem_limit_bytes=52 * 1024 * 1024),
        cost_estimate=cost(2),
        name="borders",
    )(initial, noise, target)


def attend_back(windows, d_mixed, d_packed):
    masks, blocks = head_masks(), head_blocks()

    def group(at, _):
        for window, (packed, weights_ref) in enumerate(windows):
            rows = slice(window * TOK, (window + 1) * TOK)
            here = lanes(at * LANES, LANES)
            queries = packed[:, here]
            keys = packed[:, lanes(C + at * LANES, LANES)]
            values = packed[:, lanes(2 * C + at * LANES, LANES)]
            d_mixed_blocks = by_head(d_mixed[rows, here], blocks)
            weights = weights_ref[at]
            d_weights = dot_nt(values, d_mixed_blocks)
            d_values = dot(weights, d_mixed_blocks)
            probs = weights.astype(F32)
            centred = d_weights - jnp.sum(d_weights * probs, axis=0, keepdims=True)
            d_scores = (probs * centred * SCALE).astype(BF16)
            d_keys = dot(d_scores, by_head(queries, blocks))
            d_queries = fold_heads(dot_tn(d_scores, keys), masks)
            d_packed[rows, here] = d_queries.astype(BF16)
            d_packed[rows, lanes(C + at * LANES, LANES)] = d_keys.astype(BF16)
            d_packed[rows, lanes(2 * C + at * LANES, LANES)] = d_values.astype(BF16)
        return 0

    lax.fori_loop(0, GROUPS, group, 0, unroll=GROUPS)


def saved_window(window, packed, weights, scaled, spread):
    rows = pl.ds(pl.multiple_of(window * TOK, TOK), TOK)
    groups = pl.ds(window * GROUPS, GROUPS)
    return packed.at[rows], weights.at[groups], scaled.at[rows], spread.at[rows]


def slope(difference):
    return difference * lax.rsqrt(difference * difference + SMOOTH * SMOOTH)


def step_back(d_next, windows, w_qkv_t, w_out_t, d_mixed, d_packed, d_normed):
    d_branch = d_next[...].astype(BF16)
    for part in range(4):
        at = slice(part * 256, (part + 1) * 256)
        d_mixed[:, at] = dot(d_branch, w_out_t[:, at]).astype(BF16)
    attend_back([window[:2] for window in windows], d_mixed, d_packed)
    for part in range(4):
        at = slice(part * 256, (part + 1) * 256)
        d_normed[:, at] = dot(d_packed[...], w_qkv_t[:, at])


def norm_back(at, d_next, windows, d_normed, gain):
    rows = slice(at, at + 32)
    _, _, scaled_ref, spread_ref = windows[at // TOK]
    inside = slice(at % TOK, at % TOK + 32)
    scaled = scaled_ref[inside, :].astype(F32)
    d_here = d_normed[rows, :]
    d_hat = d_here * gain
    spread = spread_ref[inside, 0:1]
    d_fields = spread * (
        d_hat
        - jnp.mean(d_hat, axis=-1, keepdims=True)
        - scaled * jnp.mean(d_hat * scaled, axis=-1, keepdims=True)
    )
    return d_next[rows, :] + d_fields, eight_rows(d_here * scaled)


def eight_rows(value):
    out = value[0:8]
    for at in range(8, value.shape[0], 8):
        out = out + value[at : at + 8]
    return out


def backward1_kernel(
    shifts_hbm,
    final,
    near,
    far,
    far_near,
    target,
    gain,
    noise,
    packed,
    weights,
    scaled,
    spread,
    w_out_t,
    w_qkv_t,
    sent,
    d_out,
    sent_out,
    head_out,
    gain_out,
    scale_out,
    shifts,
    ext,
    d_next,
    d_mixed,
    d_packed,
    d_normed,
    sems,
):
    small = start_copies(sems, 0, [(shifts_hbm, shifts)])
    me = member_index()
    for other_bits, held in enumerate((sent, near, far, far_near)):
        theirs = quarter(me ^ other_bits)
        part = held[ROWS:SENT_ROWS, :].astype(F32)
        for at in range(4):
            d_next[at * PART_ROWS : (at + 1) * PART_ROWS, theirs] = part[
                :, at * QUARTER : (at + 1) * QUARTER
            ]
    fill(ext, target, d_next[0:TOK, :], 0)
    wait_all(small)
    for row in range(LAT):
        part = frame(ext, row, shifts[1, 1], 16)
        for window in range(2):
            d_normed[window_rows(window, row), :] = part[window * WIN : (window + 1) * WIN]
    scale_total = jnp.zeros((8, C), F32)
    for at in range(0, ROWS, 32):
        rows = slice(at, at + 32)
        here = final[rows, :]
        pairs = (
            slope(here - near[rows, :].astype(F32))
            + slope(here - far[rows, :].astype(F32))
            + slope(here - far_near[rows, :].astype(F32))
        )
        seed = slope(here - d_normed[rows, :]) - pairs * (1.0 / 3.0)
        d_next[rows, :] = seed
        scale_total = scale_total + eight_rows(seed * noise[1, rows, :])
    windows = [saved_window(at, packed, weights, scaled, spread) for at in range(2)]
    step_back(d_next, windows, w_qkv_t, w_out_t, d_mixed, d_packed, d_normed)
    gain_total = jnp.zeros((8, C), F32)
    for at in range(0, ROWS, 32):
        rows = slice(at, at + 32)
        d_here, gain_part = norm_back(at, d_next, windows, d_normed, gain[...])
        d_out[rows, :] = d_here
        gain_total = gain_total + gain_part
        scale_total = scale_total + eight_rows(d_here * noise[0, rows, :])
    gain_out[...] = gain_total
    scale_out[...] = scale_total
    first = [d_out[window_rows(0, row), :] for row in range(LAT)]
    second = [d_out[window_rows(1, row), :] for row in range(LAT)]
    head_out[...] = jnp.concatenate([part[:TO_WEST] for part in first]).astype(BF16)
    skipped = 16 - TO_EAST
    sent_out[...] = jnp.concatenate(
        [part for row in range(LAT) for part in (first[row][skipped:], second[row])]
    ).astype(BF16)


def inner_window(shifts):
    return jnp.where(shifts[0, 1] >= shifts[1, 1], 1, 2)


def backward0_inner_kernel(
    shifts_hbm,
    gain,
    packed,
    weights,
    scaled,
    spread,
    w_out_t,
    w_qkv_t,
    d_in,
    gain_in,
    d_out,
    gain_out,
    shifts,
    ext,
    d_next,
    d_mixed,
    d_packed,
    d_normed,
    sems,
):
    small = start_copies(sems, 0, [(shifts_hbm, shifts)])
    for row in range(LAT):
        ext[row, 0:8, :] = d_in[row * WIN : (row + 1) * WIN, :]
        ext[row, 8:16, :] = d_in[TOK + row * WIN : TOK + (row + 1) * WIN, :]
    wait_all(small)
    window = inner_window(shifts)
    start = shifts[0, 1] - shifts[1, 1] + (window - 1) * WIN
    for row in range(LAT):
        d_next[row * WIN : (row + 1) * WIN, :] = frame(ext, row, start, WIN)
    windows = [saved_window(window, packed, weights, scaled, spread)]
    step_back(d_next, windows, w_qkv_t, w_out_t, d_mixed, d_packed, d_normed)
    gain_total = gain_in[...]
    for at in range(0, TOK, 32):
        d_here, gain_part = norm_back(at, d_next, windows, d_normed, gain[...])
        d_out[at : at + 32, :] = d_here
        gain_total = gain_total + gain_part
    gain_out[...] = gain_total


def backward0_outer_kernel(
    shifts_hbm,
    gain,
    packed,
    weights,
    scaled,
    spread,
    w_out_t,
    w_qkv_t,
    d_in,
    d_west,
    d_east,
    d_inner,
    gain_in,
    scale_in,
    own_out,
    sums_out,
    shifts,
    ext,
    d_next,
    d_mixed,
    d_packed,
    d_normed,
    sems,
):
    small = start_copies(sems, 0, [(shifts_hbm, shifts)])
    west, east = d_west[...].astype(F32), d_east[...].astype(F32)
    for row in range(LAT):
        here = slice(row * WIN, (row + 1) * WIN)
        there = slice(TOK + row * WIN, TOK + (row + 1) * WIN)
        ext[row, 16 - TO_EAST : 16, :] = west[row * TO_EAST : (row + 1) * TO_EAST]
        ext[row, 16:24, :] = d_in[here, :]
        ext[row, 24:32, :] = d_in[there, :]
        ext[row, 32 : 32 + TO_WEST, :] = east[row * TO_WEST : (row + 1) * TO_WEST]
    wait_all(small)
    lon0 = shifts[0, 1]
    inner = inner_window(shifts)
    picked = [0, 3 - inner]
    start = lon0 - shifts[1, 1] + WIN
    for row in range(LAT):
        for place, window in enumerate(picked):
            d_next[window_rows(place, row), :] = frame_of_eight(ext, row, start + window * WIN)
    windows = [saved_window(window, packed, weights, scaled, spread) for window in picked]
    step_back(d_next, windows, w_qkv_t, w_out_t, d_mixed, d_packed, d_normed)
    gain_total = gain_in[...]
    for at in range(0, ROWS, 32):
        d_here, gain_part = norm_back(at, d_next, windows, d_normed, gain[...])
        d_normed[at : at + 32, :] = d_here
        if at >= TOK:
            gain_total = gain_total + gain_part
    sums = [jnp.sum(total, axis=0, keepdims=True) for total in (gain_total, scale_in[...])]
    sums = jnp.concatenate(
        [part[:, at : at + 128] for part in sums for at in range(0, C, 128)]
    ).astype(BF16)
    for copy in range(sums_out.shape[0]):
        sums_out[copy] = sums
    first = inner == 1
    for row in range(LAT):
        done = d_inner[row * WIN : (row + 1) * WIN, :]
        rest = d_normed[window_rows(1, row), :]
        ext[row, 0:8, :] = d_normed[window_rows(0, row), :]
        ext[row, 8:16, :] = jnp.where(first, done, rest)
        ext[row, 16:24, :] = jnp.where(first, rest, done)
        own_out[row] = frame(ext, row, WIN - lon0, 16)


WORK = [
    ((LAT, 24, C), F32),
    ((ROWS, C), F32),
    ((ROWS, C), BF16),
    ((ROWS, 3 * C), BF16),
    ((ROWS, C), F32),
]
SUMS = [((8, C), F32)] * 2


def backward1(shifts, final, sent, others, target, noise, held, gain, w_qkv_t, w_out_t):
    return pl.pallas_call(
        backward1_kernel,
        out_shape=shapes(
            [((ROWS, C), F32), ((LAT * TO_EAST, C), BF16), ((LAT * TO_WEST, C), BF16)] + SUMS
        ),
        in_specs=[hbm()] + [vmem()] * 14,
        out_specs=[vmem()] * 5,
        scratch_shapes=shifts_buffers() + buffers(WORK) + [pltpu.SemaphoreType.DMA((1,))],
        compiler_params=compiler_params(),
        cost_estimate=cost(6),
        name="backward1",
    )(shifts, final, *others, target, gain, noise, *held, w_out_t, w_qkv_t, sent)


def backward0_buffers(windows, columns):
    rows = windows * TOK
    return (
        shifts_buffers()
        + buffers(
            [
                ((LAT, columns, C), F32),
                ((rows, C), F32),
                ((rows, C), BF16),
                ((rows, 3 * C), BF16),
                ((rows, C), F32),
            ]
        )
        + [pltpu.SemaphoreType.DMA((1,))]
    )


def backward0_inner(shifts, d_in, held, gain, gain_in, w_qkv_t, w_out_t):
    return pl.pallas_call(
        backward0_inner_kernel,
        out_shape=shapes([((TOK, C), F32), ((8, C), F32)]),
        in_specs=[hbm()] + [vmem()] * 9,
        out_specs=[vmem()] * 2,
        scratch_shapes=backward0_buffers(1, 16),
        compiler_params=compiler_params(),
        cost_estimate=cost(4),
        name="backward0_inner",
    )(shifts, gain, *held, w_out_t, w_qkv_t, d_in, gain_in)


def backward0_outer(copies, shifts, d_parts, held, gain, sums_in, w_qkv_t, w_out_t):
    return pl.pallas_call(
        backward0_outer_kernel,
        out_shape=shapes([((LAT, 16, C), F32), ((copies, 16, 128), BF16)]),
        in_specs=[hbm()] + [vmem()] * 13,
        out_specs=[vmem()] * 2,
        scratch_shapes=backward0_buffers(2, 40),
        compiler_params=compiler_params(),
        cost_estimate=cost(5),
        name="backward0_outer",
    )(shifts, gain, *held, w_out_t, w_qkv_t, *d_parts, *sums_in)


MEMBER = ("pair", "core")
TILE = ("far", "row", "half")


def along(value, steps):
    count = lax.axis_size(TILE)
    return lax.ppermute(value, TILE, [(at, (at + steps) % count) for at in range(count)])


def other(value, axis):
    return lax.ppermute(value, axis, [(0, 1), (1, 0)])


def total_over(copies, axes, groups=None):
    parts = lax.all_to_all(copies, axes, 0, 0, axis_index_groups=groups)
    return jnp.sum(parts.astype(F32), axis=0)


def local(initial, target, noise, w_qkv, w_out, gain, noise_scale, shifts):
    initial, noise = initial[0], noise[:, 0]
    gain_row, scale_row = gain[None], noise_scale[None]
    east, west, initial, noise, target = borders(initial, noise, target)
    east, west = along(east, -1), along(west, 1)
    prepared = prepare(w_qkv, w_out)
    east, west, prepared = lax.optimization_barrier((east, west, prepared))
    here, here_t = prepared[:2], prepared[2:]
    before, *saved0 = forward0(shifts, initial, east, west, gain_row, *here)
    sent, final, noise_here, *saved1 = forward1(
        shifts, before, noise, east, gain_row, scale_row, *here
    )
    far = other(sent, "pair")
    near = other(sent, "core")
    far_near = other(far, "core")
    d_one, d_sent, head, gain_part, scale_part = backward1(
        shifts,
        final,
        sent,
        (near, far, far_near),
        target,
        noise_here,
        saved1,
        gain_row,
        *here_t,
    )
    d_east, d_west = along(head, -1), along(d_sent, 1)
    d_inner, gain_part = backward0_inner(shifts, d_one, saved0, gain_row, gain_part, *here_t)
    near_axes = MEMBER + TILE[1:]
    state_grad, sums = backward0_outer(
        lax.axis_size(near_axes),
        shifts,
        (d_one, d_west, d_east, d_inner),
        saved0,
        gain_row,
        (gain_part, scale_part),
        *here_t,
    )
    near = lax.axis_size(near_axes)
    sums = total_over(sums, near_axes, [list(range(near))[::-1]]).astype(BF16)
    count = lax.axis_size(TILE[0])
    sums = jnp.broadcast_to(sums[None], (count,) + sums.shape)
    sums = total_over(sums, TILE[0], [[4, 5, 3, 6, 2, 7, 1, 0]]).reshape(2, C)
    members = lax.axis_size(MEMBER)
    factor = (members * LAT * initial.shape[1] * lax.axis_size(TILE)) ** (-0.5)
    return (state_grad[None], sums[0] * factor, sums[1] * factor)


def solution(mesh):
    members, tiles = mesh.devices.shape
    fine = Mesh(mesh.devices.reshape(members // 2, 2, tiles // 8, 4, 2), MEMBER + TILE)
    in_specs = (
        P(MEMBER, None, TILE, None),
        P(None, TILE, None),
        P(None, MEMBER, None, TILE, None),
        P(),
        P(),
        P(),
        P(),
        P(),
    )
    out_specs = (P(MEMBER, None, TILE, None), P(), P())
    return jax.shard_map(local, mesh=fine, in_specs=in_specs, out_specs=out_specs, check_vma=False)
```
